256 devices in a mesh: ctx: 64 (over x, y_lo, z), tp: 4 (over y_hi, core).
Axes of the slice: x: 4, y: 4 (y_hi: 2, y_lo: 2; y = y_hi * 2 + y_lo), z: 8, core: 2. Of those that a mesh axis runs over, the one named last changes fastest.
Arguments:
- queries: bfloat16 [12288, 4096], P('ctx', 'tp'), may hold values from -40 to 40
- prompt_window_keys: bfloat16 [12288, 512], P('ctx', 'tp'), may hold values from -10 to 10
- prompt_window_values: bfloat16 [12288, 512], P('ctx', 'tp'), may hold values from -6 to 6
- stored_keys: bfloat16 [4096, 512], P('ctx', 'tp'), may hold values from -4 to 4
- stored_values: bfloat16 [4096, 512], P('ctx', 'tp'), may hold values from -6 to 6
- block_order: int32 [128], replicated, may hold values from 0 to 127, as said below
- window_offset: int32 [1], replicated, may hold values from 1024 to 4096
- out_weight: bfloat16 [4096, 4096], P('tp'), may hold values from -0.25 to 0.25
Outputs:
- projected: bfloat16 [12288, 4096], P(('ctx', 'tp'))
The draws below stay inside these ranges and needn't reach their ends.
Inputs may be any that keep to these rules, and one draw needn't show every extreme that they name: `block_order`: block slots 2d and 2d + 1 (the rows of index d of ctx) hold two window blocks whose numbers add up to 127; every block appears once.
All inputs are finite; a program needn't handle non-finite values.
Results may differ from the reference program's by a relative error of at most 0.015.
Values may be sent and summed in bfloat16 or wider, within the bound.
No kernel may reach another device: no remote copies, remote signals or barrier semaphores. Data moves between devices by JAX's collectives and lax.ppermute only.
A program may use at most 64 MiB of HBM per device.

```python
import jax
import jax.numpy as jnp
from jax import lax

TOKENS_PER_PART = 192
QUERY_HEADS = 32
KEY_VALUE_HEADS = 4
HEAD_SIZE = 128
DM = 4096
BLK = 96
WINDOW_TOKENS = 12288
CACHE_SLOTS = 4096
N_CTX = 64


def shared_keys(key):
    unshaped_keys = jax.random.normal(key, (WINDOW_TOKENS, KEY_VALUE_HEADS * HEAD_SIZE), jnp.float32)
    return jnp.clip(unshaped_keys, -4.0, 4.0)


def draw_prompt_window_keys(key, part):
    base_keys = shared_keys(key)
    return base_keys.astype(jnp.bfloat16)


def draw_queries(key, part):
    key = jax.random.fold_in(key, 2)
    own_rows = jnp.clip(jax.random.normal(key, (WINDOW_TOKENS, QUERY_HEADS * HEAD_SIZE), jnp.float32), -4.0, 4.0) * 2.5
    return own_rows.astype(jnp.bfloat16)


def draw_block_order(key, part):
    key = jax.random.fold_in(key, 3)
    pair_key, flip_key = jax.random.split(key)
    pair_ids = jax.random.permutation(pair_key, N_CTX).astype(jnp.int32)
    flip_bits = jax.random.randint(flip_key, (N_CTX,), 0, 2).astype(jnp.int32)
    first_block = jnp.where(flip_bits == 0, pair_ids, 2 * N_CTX - 1 - pair_ids)
    second_block = 2 * N_CTX - 1 - first_block
    return jnp.stack([first_block, second_block], 1).reshape(2 * N_CTX).astype(jnp.int32)


def steps_of(stream_key, extent, pieces, least, largest):
    def one(axis_at, blocks):
        draws = jax.random.uniform(jax.random.fold_in(jax.random.fold_in(stream_key, 6), axis_at), (blocks,), jnp.float32, least / len(pieces), largest / len(pieces))
        return jnp.repeat(jnp.exp(draws), extent[axis_at] // blocks).reshape((-1,) + (1,) * (len(extent) - axis_at - 1))

    level = one(*pieces[0])
    for cut in pieces[1:]:
        level = level * one(*cut)
    return level


def gaussian(own_key, dims, scale, bound, shards=(), held_as=jnp.bfloat16):
    result = scale * jax.random.normal(own_key, dims, jnp.float32)
    if shards:
        result = result * steps_of(own_key, dims, shards, -0.22, 0.18)
    return jnp.clip(result, -bound, bound).astype(held_as)


def setup_inputs(seed: int = 0) -> dict:
    arg_keys = jax.random.split(jax.random.key(seed), 9)
    return {
        "queries": draw_queries(jax.random.fold_in(arg_keys[8], 71), 0),
        "prompt_window_keys": draw_prompt_window_keys(jax.random.fold_in(arg_keys[8], 71), 0),
        "prompt_window_values": gaussian(arg_keys[2], (WINDOW_TOKENS, KEY_VALUE_HEADS * HEAD_SIZE), 1.0, 6.0, ((0, 64), (1, 4))),
        "stored_keys": gaussian(arg_keys[3], (CACHE_SLOTS, KEY_VALUE_HEADS * HEAD_SIZE), 1.0, 4.0, ((0, 64), (1, 4))),
        "stored_values": gaussian(arg_keys[4], (CACHE_SLOTS, KEY_VALUE_HEADS * HEAD_SIZE), 1.0, 6.0, ((0, 64), (1, 4))),
        "block_order": draw_block_order(jax.random.fold_in(arg_keys[8], 71), 0),
        "window_offset": jax.random.randint(arg_keys[6], (1,), CACHE_SLOTS // 4, CACHE_SLOTS + 1).astype(jnp.int32),
        "out_weight": gaussian(arg_keys[7], (QUERY_HEADS * HEAD_SIZE, DM), (QUERY_HEADS * HEAD_SIZE // 8) ** -0.5, 0.25, ((0, 4),)),
    }


def reference(queries, prompt_window_keys, prompt_window_values, stored_keys, stored_values, block_order, window_offset, out_weight):
    group_split = QUERY_HEADS // KEY_VALUE_HEADS
    score_scale = HEAD_SIZE ** -0.5
    row_index = jnp.arange(WINDOW_TOKENS, dtype=jnp.int32)
    positions = block_order[row_index // BLK] * BLK + row_index % BLK
    cache_visible = jnp.arange(CACHE_SLOTS, dtype=jnp.int32) < window_offset[0]
    keys_combined = jnp.concatenate([prompt_window_keys, stored_keys], 0).reshape(WINDOW_TOKENS + CACHE_SLOTS, KEY_VALUE_HEADS, HEAD_SIZE).astype(jnp.float32)
    values_combined = jnp.concatenate([prompt_window_values, stored_values], 0).reshape(WINDOW_TOKENS + CACHE_SLOTS, KEY_VALUE_HEADS, HEAD_SIZE).astype(jnp.float32)

    def one_device(device):
        first_row = (device * TOKENS_PER_PART).astype(jnp.int32)
        query_matrix = lax.dynamic_slice_in_dim(queries, first_row, TOKENS_PER_PART, 0)
        query_matrix = query_matrix.reshape(TOKENS_PER_PART, KEY_VALUE_HEADS, group_split, HEAD_SIZE).astype(jnp.float32)
        query_pos = lax.dynamic_slice_in_dim(positions, first_row, TOKENS_PER_PART, 0)
        visible = jnp.concatenate([positions[None, :] <= query_pos[:, None], jnp.broadcast_to(cache_visible[None, :], (TOKENS_PER_PART, CACHE_SLOTS))], 1)

        def single_group(group_index):
            query_group = lax.dynamic_index_in_dim(query_matrix, group_index, 1, keepdims=False)
            key_group = lax.dynamic_index_in_dim(keys_combined, group_index, 1, keepdims=False)
            value_group = lax.dynamic_index_in_dim(values_combined, group_index, 1, keepdims=False)
            scores = jnp.einsum("tgd,nd->tgn", query_group, key_group, precision=lax.Precision.HIGHEST) * score_scale
            scores = jnp.where(visible[:, None, :], scores, -jnp.inf)
            row_max = jnp.max(scores, axis=-1, keepdims=True)
            weights = jnp.exp(scores - row_max)
            row_total = jnp.sum(weights, axis=-1, keepdims=True)
            rounded = lax.optimization_barrier(weights.astype(jnp.bfloat16)).astype(jnp.float32)
            mixed = jnp.einsum("tgn,nd->tgd", rounded, value_group, precision=lax.Precision.HIGHEST)
            return mixed / row_total

        head_split = lax.map(single_group, jnp.arange(KEY_VALUE_HEADS, dtype=jnp.int32))
        return jnp.transpose(head_split, (1, 0, 2, 3)).reshape(TOKENS_PER_PART, QUERY_HEADS * HEAD_SIZE).astype(jnp.bfloat16)

    attended = lax.map(one_device, jnp.arange(N_CTX, dtype=jnp.int32)).reshape(WINDOW_TOKENS, QUERY_HEADS * HEAD_SIZE)
    return jnp.dot(attended, out_weight, preferred_element_type=jnp.float32).astype(jnp.bfloat16)
```

```python
import functools

import jax
import jax.numpy as jnp
from jax import lax
from jax.experimental import pallas as pl
from jax.experimental.pallas import tpu as pltpu
from jax.sharding import Mesh, PartitionSpec as P

HEADS = 8
D = 128
BLK = 96
TOK = 2 * BLK
CACHE = 64
SHARD = 2 * (TOK + CACHE)
ROWS = HEADS * BLK
TILE = 512
NEG = -1e30
SCALE = D**-0.5 * 1.4426950408889634
OUT_ROWS = D + 16
NT = (((1,), (1,)), ((), ()))
TN = (((0,), (0,)), ((), ()))
VMEM = pltpu.VMEM


def attend_chunk(steps, first, last, *refs):
    refs = list(refs)
    place_ref, order_ref = refs[:2]
    q_refs = refs[2:6]
    msgs = refs[6 : 6 + len(steps)]
    refs = refs[6 + len(steps) :]
    if not first:
        m_in, l_in, acc_in = refs[:3]
        refs = refs[3:]
    if last:
        outs = refs[:4]
        refs = refs[4:]
    else:
        m_out, l_out, acc_out = refs[:3]
        refs = refs[3:]
    qx, kx, vx, s_a, s_b, m_s, l_s, acc_s, where = refs
    x, yl, z, offset = place_ref[0], place_ref[1], place_ref[2], place_ref[3]
    n_blocks = 4 * len(steps)

    token = lax.broadcasted_iota(jnp.int32, (BLK, D), 0)
    column = lax.broadcasted_iota(jnp.int32, (BLK, D), 1)
    hidden = ((column < BLK) & (column > token)) | (column == BLK)
    q_extra = jnp.where(hidden, NEG, 0.0).astype(jnp.bfloat16)
    own_rows = jnp.where(column == token, 1.0, 0.0).astype(jnp.bfloat16)
    for g in range(4):
        for b in range(2):
            for h in range(HEADS):
                rows = slice(h * BLK, (h + 1) * BLK)
                qx[2 * g + b, rows, :D] = q_refs[g][b * BLK : (b + 1) * BLK, h * D : (h + 1) * D]
                qx[2 * g + b, rows, D:] = q_extra
    kx[...] = jnp.zeros_like(kx)
    vx[...] = jnp.zeros_like(vx)

    ctxs = []
    for step in steps:
        zz = lax.rem(z + step + 8, 8)
        ctxs += [x * 16 + yl * 8 + zz, (3 - x) * 16 + yl * 8 + zz]
    cache_rows = jnp.int32(0)
    slot = lax.broadcasted_iota(jnp.int32, (CACHE, D), 0)
    lane = lax.broadcasted_iota(jnp.int32, (CACHE, D), 1)
    for j, ctx in enumerate(ctxs):
        filled = offset - ctx * CACHE
        src = msgs[j // 2]
        base = (j % 2) * SHARD

        @pl.when(filled > 0)
        def _(src=src, base=base, at=cache_rows, filled=filled):
            to = pl.ds(pl.multiple_of(at, CACHE), CACHE)
            kx[to, :D] = src[base + TOK : base + TOK + CACHE, :]
            kx[to, D:] = jnp.where((slot >= filled) & (lane == BLK), 1.0, 0.0).astype(jnp.bfloat16)
            vx[to, :] = src[base + 2 * TOK + CACHE : base + SHARD, :]

        cache_rows = cache_rows + jnp.where(filled > 0, CACHE, 0)

    ids = [order_ref[2 * ctx + b] for ctx in ctxs for b in range(2)]
    for j, mine in enumerate(ids):
        where[j] = mine
        rank = jnp.int32(0)
        for k, other in enumerate(ids):
            if k != j:
                rank = rank + (other < mine).astype(jnp.int32)
        to = pl.ds(pl.multiple_of(cache_rows + rank * BLK, 32), BLK)
        src = msgs[j // 4]
        base = ((j // 2) % 2) * SHARD + (j % 2) * BLK
        kx[to, :D] = src[base : base + BLK, :]
        vx[to, :] = src[base + TOK + CACHE : base + TOK + CACHE + BLK, :]

    pad_lane = lax.broadcasted_iota(jnp.int32, (TILE, D), 1)
    pad_rows = jnp.where(pad_lane == BLK, 1.0, 0.0).astype(jnp.bfloat16)

    def scores(qb, i):
        keys = kx[pl.ds(pl.multiple_of(i * TILE, TILE), TILE), :]
        return lax.dot_general(keys, qx[qb], NT, preferred_element_type=jnp.float32)

    def absorb(s_ref, i):
        s = s_ref[...]
        m0 = m_s[...]
        m1 = jnp.maximum(m0, jnp.max(s, axis=0, keepdims=True) * SCALE)
        factor = jnp.exp2(m0 - m1)
        p = jnp.exp2(s * SCALE - m1[:1])
        l_s[...] = l_s[...] * factor + jnp.sum(p, axis=0, keepdims=True)
        m_s[...] = m1
        values = vx[pl.ds(pl.multiple_of(i * TILE, TILE), TILE), :]
        acc_s[...] = acc_s[...] * factor[:1] + lax.dot_general(
            values, p.astype(jnp.bfloat16), TN, preferred_element_type=jnp.float32
        )

    def block(qb, carry):
        g, b = qb // 2, qb % 2
        gx, gy = g % 2, g // 2
        q_ctx = (x + gx - 2 * gx * lax.rem(x, 2)) * 16 + (yl + gy - 2 * gy * yl) * 8 + z
        q_id = order_ref[2 * q_ctx + b]
        count = jnp.int32(0)
        own = jnp.int32(0)
        for j in range(n_blocks):
            count = count + (where[j] <= q_id).astype(jnp.int32)
            own = own + (where[j] == q_id).astype(jnp.int32)
        end = cache_rows + count * BLK
        tiles = (end + TILE - 1) // TILE
        if first:
            m_s[...] = jnp.full_like(m_s, NEG)
            l_s[...] = jnp.zeros_like(l_s)
            acc_s[...] = jnp.zeros_like(acc_s)
        else:
            m_s[...] = m_in[qb]
            l_s[...] = l_in[qb]
            acc_s[...] = acc_in[qb]
        tail = pl.ds(pl.multiple_of(end, 32), TILE)
        kx[tail, D:] = pad_rows

        @pl.when(own > 0)
        def _():
            kx[pl.ds(pl.multiple_of(jnp.maximum(end - BLK, 0), 32), BLK), D:] = own_rows

        @pl.when(tiles > 0)
        def _():
            s_a[...] = scores(qb, 0)

            def pair(j, c):
                i = 2 * j
                s_b[...] = scores(qb, i + 1)
                absorb(s_a, i)
                s_a[...] = scores(qb, i + 2)
                absorb(s_b, i + 1)
                return c

            lax.fori_loop(0, (tiles - 1) // 2, pair, 0)

            @pl.when(tiles % 2 == 0)
            def _():
                s_b[...] = scores(qb, tiles - 1)
                absorb(s_a, tiles - 2)
                absorb(s_b, tiles - 1)

            @pl.when(tiles % 2 == 1)
            def _():
                absorb(s_a, tiles - 1)

        kx[tail, D:] = jnp.zeros_like(pad_rows)

        @pl.when(own > 0)
        def _():
            kx[pl.ds(pl.multiple_of(jnp.maximum(end - BLK, 0), 32), BLK), D:] = jnp.zeros_like(own_rows)

        if last:
            total = l_s[...]
            some = total > 0.0
            safe = jnp.where(some, total, 1.0)
            value = (acc_s[...] / safe[:1]).astype(jnp.bfloat16)
            logsum = jnp.where(some, m_s[...] + jnp.log2(safe), NEG)
            high = logsum.astype(jnp.bfloat16)
            rest = logsum - high.astype(jnp.float32)
            mid = rest.astype(jnp.bfloat16)
            low = (rest - mid.astype(jnp.float32)).astype(jnp.bfloat16)
            row = lax.broadcasted_iota(jnp.int32, (16, ROWS), 0)
            h2 = jnp.concatenate([high, high], 0).astype(jnp.float32)
            m2 = jnp.concatenate([mid, mid], 0).astype(jnp.float32)
            l2 = jnp.concatenate([low, low], 0).astype(jnp.float32)
            pieces = jnp.where(row == 0, h2, jnp.where(row == 1, m2, l2)).astype(jnp.bfloat16)
            for gg in range(4):

                @pl.when(g == gg)
                def _(gg=gg):
                    outs[gg][b, :D, :] = value
                    outs[gg][b, D:, :] = pieces
        else:
            m_out[qb] = m_s[...]
            l_out[qb] = l_s[...]
            acc_out[qb] = acc_s[...]
        return carry

    lax.fori_loop(0, 8, block, 0)


def run_chunk(steps, state, last, place, order, queries, messages):
    first = state is None
    keep = 256 * 2 * len(steps) + TILE
    sds = jax.ShapeDtypeStruct
    state_shapes = (
        sds((8, 8, ROWS), jnp.float32),
        sds((8, 8, ROWS), jnp.float32),
        sds((8, D, ROWS), jnp.float32),
    )
    smem = pl.BlockSpec(memory_space=pltpu.SMEM)
    vmem = pl.BlockSpec(memory_space=VMEM)
    operands = [place, order, *queries, *messages] + ([] if first else list(state))
    out_shape = (sds((2, OUT_ROWS, ROWS), jnp.bfloat16),) * 4 if last else state_shapes
    work = 2 * len(steps)
    aliases = {}
    if not first and not last:
        aliases = {len(operands) - 3 + i: i for i in range(3)}
    return pl.pallas_call(
        functools.partial(attend_chunk, tuple(steps), first, last),
        out_shape=out_shape,
        in_specs=[smem, smem] + [vmem] * (len(operands) - 2),
        out_specs=(vmem,) * len(out_shape),
        scratch_shapes=[
            VMEM((8, ROWS, 2 * D), jnp.bfloat16),
            VMEM((keep, 2 * D), jnp.bfloat16),
            VMEM((keep, D), jnp.bfloat16),
            VMEM((TILE, ROWS), jnp.float32),
            VMEM((TILE, ROWS), jnp.float32),
            VMEM((8, ROWS), jnp.float32),
            VMEM((8, ROWS), jnp.float32),
            VMEM((D, ROWS), jnp.float32),
            pltpu.SMEM((2 * work,), jnp.int32),
        ],
        input_output_aliases=aliases,
        compiler_params=pltpu.CompilerParams(vmem_limit_bytes=48 * 2**20),
        cost_estimate=pl.CostEstimate(
            flops=work * 1024 * 1024 * 1024, bytes_accessed=8 * 2**20, transcendentals=work * 10**6
        ),
        name=f"attend_{len(steps)}_{int(first)}{int(last)}",
    )(*operands)


def merge_body(*refs):
    parts, out = refs[:4], refs[4]
    for b in range(2):
        logs = []
        for part in parts:
            row = part[b, D:, :].astype(jnp.float32)
            logs.append(row[0:1] + row[1:2] + row[2:3])
        top = functools.reduce(jnp.maximum, logs)
        weights = [jnp.exp2(v - top) for v in logs]
        share = 1.0 / sum(weights)
        mixed = sum(part[b, :D, :].astype(jnp.float32) * (w * share) for part, w in zip(parts, weights))
        for h in range(HEADS):
            out[b * BLK : (b + 1) * BLK, h * D : (h + 1) * D] = mixed[:, h * BLK : (h + 1) * BLK].T.astype(
                jnp.bfloat16
            )


def merge(parts):
    vmem = pl.BlockSpec(memory_space=VMEM)
    return pl.pallas_call(
        merge_body,
        out_shape=jax.ShapeDtypeStruct((TOK, HEADS * D), jnp.bfloat16),
        in_specs=[vmem] * 4,
        out_specs=vmem,
        name="merge",
    )(*parts)


def on_device(queries, window_keys, window_values, stored_keys, stored_values, block_order, window_offset, out_weight):
    x, yl, z = lax.axis_index("x"), lax.axis_index("yl"), lax.axis_index("z")
    place = jnp.stack([x, yl, z, window_offset[0]]).astype(jnp.int32)
    shard = jnp.concatenate([window_keys, stored_keys, window_values, stored_values], 0)

    def along(array, axis, size, to):
        return lax.ppermute(array, axis, [(i, to(i)) for i in range(size)])

    other = along(shard, "x", 4, lambda i: 3 - i)
    base = jnp.concatenate([shard, other], 0)
    pair = [(a, b) for a in range(4) for b in range(2)]
    both = [(2 * a + b, 2 * (a ^ 1) + (1 - b)) for a, b in pair]
    q_sets = [
        queries,
        along(queries, "x", 4, lambda i: i ^ 1),
        along(queries, "yl", 2, lambda i: 1 - i),
        lax.ppermute(queries, ("x", "yl"), both),
    ]
    up = lambda a: along(a, "z", 8, lambda i: (i + 1) % 8)
    down = lambda a: along(a, "z", 8, lambda i: (i - 1) % 8)
    a1, b1 = up(base), down(base)
    a2, b2 = up(a1), down(b1)
    a3, b3 = up(a2), down(b2)
    far = jnp.concatenate([up(a3[:SHARD]), down(b3[SHARD:])], 0)
    state = run_chunk((0, -1, 1), None, False, place, block_order, q_sets, (base, a1, b1))
    state = run_chunk((-2, 2, -3, 3), state, False, place, block_order, q_sets, (a2, b2, a3, b3))
    parts = run_chunk((4,), state, True, place, block_order, q_sets, (far,))
    parts = [
        parts[0],
        along(parts[1], "x", 4, lambda i: i ^ 1),
        along(parts[2], "yl", 2, lambda i: 1 - i),
        lax.ppermute(parts[3], ("x", "yl"), both),
    ]
    attended = merge(parts)
    partial = jnp.dot(attended, out_weight, preferred_element_type=jnp.float32).reshape(2, 2, TOK // 4, -1)
    core, yh = lax.axis_index("core"), lax.axis_index("yh")
    give = lax.dynamic_index_in_dim(partial, 1 - core, 1, keepdims=False).astype(jnp.bfloat16)
    mine = lax.dynamic_index_in_dim(partial, core, 1, keepdims=False)
    mine = mine + along(give, "core", 2, lambda i: 1 - i).astype(jnp.float32)
    give = lax.dynamic_index_in_dim(mine, 1 - yh, 0, keepdims=False).astype(jnp.bfloat16)
    mine = lax.dynamic_index_in_dim(mine, yh, 0, keepdims=False)
    return (mine + along(give, "yh", 2, lambda i: 1 - i).astype(jnp.float32)).astype(jnp.bfloat16)


def solution(mesh):
    fine = Mesh(mesh.devices.reshape(4, 2, 8, 2, 2), ("x", "yl", "z", "yh", "core"))
    ctx, tp = ("x", "yl", "z"), ("yh", "core")
    return jax.shard_map(
        on_device,
        mesh=fine,
        in_specs=(P(ctx, tp),) * 5 + (P(), P(), P(tp, None)),
        out_specs=P((*ctx, *tp), None),
        check_vma=False,
    )
```

```python
import functools

import jax
import jax.numpy as jnp
from jax import lax
from jax.experimental import pallas as pl
from jax.experimental.pallas import tpu as pltpu
from jax.sharding import Mesh, PartitionSpec as P

HEADS = 8
D = 128
BLK = 96
TOK = 2 * BLK
CACHE = 64
SHARD = 2 * (TOK + CACHE)
ROWS = HEADS * BLK
TILE = 512
NEG = -1e30
SCALE = D**-0.5 * 1.4426950408889634
PLACE = 128
OUT_ROWS = D + 16
NT = (((1,), (1,)), ((), ()))
TN = (((0,), (0,)), ((), ()))
VMEM = pltpu.VMEM


def attend_chunk(work, sets, steps, first, last, *refs):
    refs = list(refs)

    def take(count):
        taken = refs[:count]
        del refs[:count]
        return taken

    n_query = len(work)
    (table_ref,) = take(1)
    q_refs = take(len(sets))
    msgs = take(len(steps))
    old = [] if first else take(3 * n_query)
    outs = take(n_query if last else 3 * n_query)
    m_all, l_all, acc_all, qx, kx, vx, s_a, s_b, ends, marks, item_block, item_tile = refs
    x, yl, z, offset, yh = (table_ref[PLACE + i] for i in (0, 1, 2, 3, 5))
    n_keys = 256 * 2 * len(steps)

    token = lax.broadcasted_iota(jnp.int32, (BLK, D), 0)
    column = lax.broadcasted_iota(jnp.int32, (BLK, D), 1)
    hidden = ((column < BLK) & (column > token)) | (column == BLK)
    q_extra = jnp.where(hidden, NEG, 0.0).astype(jnp.bfloat16)
    own_rows = jnp.where(column == token, 1.0, 0.0).astype(jnp.bfloat16)
    half_of = [yh if role else 1 - yh for _, role in work]
    for qb, (g, role) in enumerate(work):
        src = q_refs[sets.index(g)]
        at = pl.ds(pl.multiple_of(half_of[qb] * BLK, 32), BLK)
        for h in range(HEADS):
            rows = slice(h * BLK, (h + 1) * BLK)
            qx[qb, rows, :D] = src[at, h * D : (h + 1) * D]
            qx[qb, rows, D:] = q_extra
    kx[:, D:] = jnp.zeros((kx.shape[0], D), jnp.bfloat16)
    kx[n_keys - 512 :, :D] = jnp.zeros((kx.shape[0] - n_keys + 512, D), jnp.bfloat16)
    vx[...] = jnp.zeros_like(vx)

    ctxs = []
    for step in steps:
        zz = lax.rem(z + step + 8, 8)
        ctxs += [x * 16 + yl * 8 + zz, (3 - x) * 16 + yl * 8 + zz]
    cache_rows = jnp.int32(0)
    slot = lax.broadcasted_iota(jnp.int32, (CACHE, D), 0)
    lane = lax.broadcasted_iota(jnp.int32, (CACHE, D), 1)
    for j, ctx in enumerate(ctxs):
        filled = offset - ctx * CACHE
        src = msgs[j // 2]
        base = (j % 2) * SHARD

        @pl.when(filled > 0)
        def _(src=src, base=base, at=cache_rows, filled=filled):
            to = pl.ds(pl.multiple_of(at, CACHE), CACHE)
            kx[to, :D] = src[base + TOK : base + TOK + CACHE, :]
            kx[to, D:] = jnp.where((slot >= filled) & (lane == BLK), 1.0, 0.0).astype(jnp.bfloat16)
            vx[to, :] = src[base + 2 * TOK + CACHE : base + SHARD, :]

        cache_rows = cache_rows + jnp.where(filled > 0, CACHE, 0)

    ids = [table_ref[2 * ctx + b] for ctx in ctxs for b in range(2)]
    for j, mine in enumerate(ids):
        rank = jnp.int32(0)
        for k, other in enumerate(ids):
            if k != j:
                rank = rank + (other < mine).astype(jnp.int32)
        to = pl.ds(pl.multiple_of(cache_rows + rank * BLK, 32), BLK)
        src = msgs[j // 4]
        base = ((j // 2) % 2) * SHARD + (j % 2) * BLK
        kx[to, :D] = src[base : base + BLK, :]
        vx[to, :] = src[base + TOK + CACHE : base + TOK + CACHE + BLK, :]

    items = jnp.int32(0)
    for qb, (g, role) in enumerate(work):
        gx, gy = g % 2, g // 2
        q_x = x + 1 - 2 * lax.rem(x, 2) if gx else x
        q_y = 1 - yl if gy else yl
        q_id = table_ref[2 * (q_x * 16 + q_y * 8 + z) + half_of[qb]]
        count = jnp.int32(0)
        own = jnp.int32(0)
        for k in ids:
            count = count + (k <= q_id).astype(jnp.int32)
            own = own + (k == q_id).astype(jnp.int32)
        end = cache_rows + count * BLK
        ends[qb] = end
        marks[qb] = jnp.where(own > 0, end - BLK, n_keys + TILE)
        tiles = (end + TILE - 1) // TILE

        def add(t, at, qb=qb):
            item_block[at] = qb
            item_tile[at] = t
            return at + 1

        items = lax.fori_loop(0, tiles, add, items)
        if first:
            m_all[qb] = jnp.full((8, ROWS), NEG, jnp.float32)
            l_all[qb] = jnp.zeros((8, ROWS), jnp.float32)
            acc_all[qb] = jnp.zeros((D, ROWS), jnp.float32)
        else:
            m_all[qb], l_all[qb], acc_all[qb] = (ref[...] for ref in old[3 * qb : 3 * qb + 3])

    pad_lane = lax.broadcasted_iota(jnp.int32, (TILE, D), 1)
    pad_rows = jnp.where(pad_lane == BLK, 1.0, 0.0).astype(jnp.bfloat16)

    def scores(k, before):
        old, new = item_block[before], item_block[k]
        kx[pl.ds(pl.multiple_of(ends[old], 32), TILE), D:] = jnp.zeros_like(pad_rows)
        kx[pl.ds(pl.multiple_of(marks[old], 32), BLK), D:] = jnp.zeros_like(own_rows)
        kx[pl.ds(pl.multiple_of(ends[new], 32), TILE), D:] = pad_rows
        kx[pl.ds(pl.multiple_of(marks[new], 32), BLK), D:] = own_rows
        keys = kx[pl.ds(pl.multiple_of(item_tile[k] * TILE, TILE), TILE), :]
        return lax.dot_general(keys, qx[new], NT, preferred_element_type=jnp.float32)

    def absorb(s_ref, k):
        qb = item_block[k]
        s = s_ref[...]
        m0 = m_all[qb]
        m1 = jnp.maximum(m0, jnp.max(s, axis=0, keepdims=True) * SCALE)
        factor = jnp.exp2(m0 - m1)
        p = jnp.exp2(s * SCALE - m1[:1])
        l_all[qb] = l_all[qb] * factor + jnp.sum(p, axis=0, keepdims=True)
        m_all[qb] = m1
        values = vx[pl.ds(pl.multiple_of(item_tile[k] * TILE, TILE), TILE), :]
        acc_all[qb] = acc_all[qb] * factor[:1] + lax.dot_general(
            values, p.astype(jnp.bfloat16), TN, preferred_element_type=jnp.float32
        )

    @pl.when(items > 0)
    def _():
        s_a[...] = scores(0, 0)

        def pair(j, c):
            k = 2 * j
            s_b[...] = scores(k + 1, k)
            absorb(s_a, k)
            s_a[...] = scores(k + 2, k + 1)
            absorb(s_b, k + 1)
            return c

        lax.fori_loop(0, (items - 1) // 2, pair, 0)

        @pl.when(items % 2 == 0)
        def _():
            s_b[...] = scores(items - 1, items - 2)
            absorb(s_a, items - 2)
            absorb(s_b, items - 1)

        @pl.when(items % 2 == 1)
        def _():
            absorb(s_a, items - 1)

    for qb in range(n_query):
        if last:
            total = l_all[qb]
            some = total > 0.0
            safe = jnp.where(some, total, 1.0)
            logsum = jnp.where(some, m_all[qb] + jnp.log2(safe), NEG)
            high = logsum.astype(jnp.bfloat16)
            rest = logsum - high.astype(jnp.float32)
            mid = rest.astype(jnp.bfloat16)
            low = (rest - mid.astype(jnp.float32)).astype(jnp.bfloat16)
            row = lax.broadcasted_iota(jnp.int32, (16, ROWS), 0)
            h2, m2, l2 = (jnp.concatenate([v, v], 0).astype(jnp.float32) for v in (high, mid, low))
            outs[qb][:D, :] = (acc_all[qb] / safe[:1]).astype(jnp.bfloat16)
            outs[qb][D:, :] = jnp.where(row == 0, h2, jnp.where(row == 1, m2, l2)).astype(jnp.bfloat16)
        else:
            for ref, kept in zip(outs[3 * qb : 3 * qb + 3], (m_all, l_all, acc_all)):
                ref[...] = kept[qb]


def run_chunk(work, steps, state, last, table, queries, messages):
    first = work[0] not in state
    sets = sorted({g for g, _ in work})
    n_query = len(work)
    n_keys = 256 * 2 * len(steps)
    keep = n_keys + TILE + 128
    max_items = n_query * (n_keys // TILE + 1) + 2
    shapes = [(8, ROWS), (8, ROWS), (D, ROWS)]
    smem = pl.BlockSpec(memory_space=pltpu.SMEM)
    vmem = pl.BlockSpec(memory_space=VMEM)
    operands = [table, *(queries[g] for g in sets), *messages]
    if not first:
        operands += [array for key in work for array in state[key]]
    if last:
        out_shape = [jax.ShapeDtypeStruct((OUT_ROWS, ROWS), jnp.bfloat16)] * n_query
    else:
        out_shape = [jax.ShapeDtypeStruct(s, jnp.float32) for s in shapes] * n_query
    pairs = n_query * n_keys * ROWS * 6 // 10
    name = "_".join(["attend", *(str(g) + "AB"[role] for g, role in work), str(len(steps))])
    results = pl.pallas_call(
        functools.partial(attend_chunk, tuple(work), tuple(sets), tuple(steps), first, last),
        out_shape=out_shape,
        in_specs=[smem] + [vmem] * (len(operands) - 1),
        out_specs=[vmem] * len(out_shape),
        scratch_shapes=[VMEM((n_query, *s), jnp.float32) for s in shapes]
        + [
            VMEM((n_query, ROWS, 2 * D), jnp.bfloat16),
            VMEM((keep, 2 * D), jnp.bfloat16),
            VMEM((keep, D), jnp.bfloat16),
            VMEM((TILE, ROWS), jnp.float32),
            VMEM((TILE, ROWS), jnp.float32),
            pltpu.SMEM((8,), jnp.int32),
            pltpu.SMEM((8,), jnp.int32),
            pltpu.SMEM((max_items,), jnp.int32),
            pltpu.SMEM((max_items,), jnp.int32),
        ],
        compiler_params=pltpu.CompilerParams(vmem_limit_bytes=24 * 2**20),
        cost_estimate=pl.CostEstimate(flops=pairs * 1024, bytes_accessed=8 * 2**20, transcendentals=pairs),
        name=name,
    )(*operands)
    if last:
        return results
    for i, key in enumerate(work):
        state[key] = tuple(results[3 * i : 3 * i + 3])
    return state


def project_body(table_ref, a_ref, b_ref, c_ref, d_ref, w_ref, give_ref, mine_ref, att):
    parts = (a_ref, b_ref, c_ref, d_ref)
    logs = []
    for part in parts:
        row = part[D:, :].astype(jnp.float32)
        logs.append(row[0:1] + row[1:2] + row[2:3])
    top = functools.reduce(jnp.maximum, logs)
    weights = [jnp.exp2(v - top) for v in logs]
    share = 1.0 / sum(weights)
    mixed = sum(part[:D, :].astype(jnp.float32) * (w * share) for part, w in zip(parts, weights))
    turned = mixed.T.astype(jnp.bfloat16)
    for h in range(HEADS):
        att[:, h * D : (h + 1) * D] = turned[h * BLK : (h + 1) * BLK, :]
    core = table_ref[PLACE + 4]
    half = BLK // 2
    wide = 512
    for c in range(w_ref.shape[1] // wide):
        cols = slice(c * wide, (c + 1) * wide)
        full = jnp.dot(att[...], w_ref[:, cols], preferred_element_type=jnp.float32)
        give_ref[:, cols] = jnp.where(core == 0, full[half:], full[:half]).astype(jnp.bfloat16)
        mine_ref[:, cols] = jnp.where(core == 0, full[:half], full[half:])


def project(table, parts, weight):
    vmem = pl.BlockSpec(memory_space=VMEM)
    wide = weight.shape[1]
    return pl.pallas_call(
        project_body,
        out_shape=(
            jax.ShapeDtypeStruct((BLK // 2, wide), jnp.bfloat16),
            jax.ShapeDtypeStruct((BLK // 2, wide), jnp.float32),
        ),
        in_specs=[pl.BlockSpec(memory_space=pltpu.SMEM)] + [vmem] * 5,
        out_specs=(vmem, vmem),
        scratch_shapes=[VMEM((BLK, HEADS * D), jnp.bfloat16)],
        compiler_params=pltpu.CompilerParams(vmem_limit_bytes=24 * 2**20),
        cost_estimate=pl.CostEstimate(flops=2 * BLK * HEADS * D * wide, bytes_accessed=12 * 2**20, transcendentals=0),
        name="project",
    )(table, *parts, weight)


def total_body(table_ref, *refs):
    mine, gathered, *others = refs[:-1]
    terms = [mine[...], gathered[1 - table_ref[PLACE + 4]], *(ref[...] for ref in others)]
    refs[-1][...] = sum(term.astype(jnp.float32) for term in terms).astype(jnp.bfloat16)


def total(table, *terms):
    vmem = pl.BlockSpec(memory_space=VMEM)
    return pl.pallas_call(
        total_body,
        out_shape=jax.ShapeDtypeStruct(terms[0].shape, jnp.bfloat16),
        in_specs=[pl.BlockSpec(memory_space=pltpu.SMEM)] + [vmem] * len(terms),
        out_specs=vmem,
        compiler_params=pltpu.CompilerParams(vmem_limit_bytes=8 * 2**20),
        name=f"total_{len(terms)}",
    )(table, *terms)


def stage_body(src, dst):
    dst[...] = src[...]


def stage(array):
    vmem = pl.BlockSpec(memory_space=VMEM)
    return pl.pallas_call(
        stage_body,
        out_shape=jax.ShapeDtypeStruct(array.shape, array.dtype),
        in_specs=[vmem],
        out_specs=vmem,
        compiler_params=pltpu.CompilerParams(vmem_limit_bytes=8 * 2**20),
        name="stage",
    )(array)


def on_device(queries, window_keys, window_values, stored_keys, stored_values, block_order, window_offset, out_weight):
    x, yl, z = lax.axis_index("x"), lax.axis_index("yl"), lax.axis_index("z")
    core, yh = lax.axis_index("core"), lax.axis_index("yh")
    place = jnp.stack([x, yl, z, window_offset[0], core, yh]).astype(jnp.int32)
    table = jnp.concatenate([block_order, place])
    shard = jnp.concatenate([window_keys, stored_keys, window_values, stored_values], 0)

    def along(array, axis, size, to):
        return lax.ppermute(array, axis, [(i, to(i)) for i in range(size)])

    shard, queries = lax.optimization_barrier((shard, queries))
    other = along(shard, "x", 4, lambda i: 3 - i)
    base = jnp.concatenate([shard, other], 0)
    pair = [(a, b) for a in range(4) for b in range(2)]
    both = [(2 * a + b, 2 * (a ^ 1) + (1 - b)) for a, b in pair]
    to_member = [
        lambda v: v,
        lambda v: along(v, "x", 4, lambda i: i ^ 1),
        lambda v: along(v, "yl", 2, lambda i: 1 - i),
        lambda v: lax.ppermute(v, ("x", "yl"), both),
    ]
    q_sets = [queries] + [to_member[g](queries) for g in (1, 2, 3)]
    up = lambda a: along(a, "z", 8, lambda i: (i + 1) % 8)
    down = lambda a: along(a, "z", 8, lambda i: (i - 1) % 8)
    base, table, q_sets[0] = lax.optimization_barrier((base, table, stage(queries)))
    a1, b1 = up(base), down(base)
    a2, b2 = up(a1), down(b1)
    state = {}
    run = lambda work, steps, messages, last=False: run_chunk(work, steps, state, last, table, q_sets, messages)
    tie = lax.optimization_barrier
    near = (0, -1, 1), (base, a1, b1)
    A, B = 0, 1
    run([(0, A), (0, B)], *near)
    run([(3, A), (3, B)], *near)
    a2, b2, state[0, A], state[3, A] = tie((a2, b2, state[0, A], state[3, A]))
    a3, b3 = up(a2), down(b2)
    far = jnp.concatenate([up(a3[:SHARD]), down(b3[SHARD:])], 0)
    run([(1, A), (1, B), (2, A), (2, B)], *near)
    run([(g, r) for r in (A, B) for g in (1, 2, 3)], (-2, 2), (a2, b2))
    end = (-3, 3, 4), (a3, b3, far)
    sent_a = run([(3, A), (1, A), (2, A)], *end, True)
    *sent_a, state[3, B] = tie((*sent_a, state[3, B]))
    got_a = [to_member[g](v) for g, v in zip((3, 1, 2), sent_a)]
    sent_b = run([(3, B), (1, B), (2, B)], *end, True)
    got_b = [to_member[g](v) for g, v in zip((3, 1, 2), sent_b)]
    *got_a, state[0, A] = tie((*got_a, state[0, A]))
    own_a, own_b = run([(0, A), (0, B)], (-2, 2, -3, 3, 4), (a2, b2, a3, b3, far), True)
    give_a, keep_a = project(table, (own_a, *got_a), out_weight)
    sum_a = total(table, keep_a, lax.all_gather(give_a, "core"))
    across = along(sum_a, "yh", 2, lambda i: 1 - i)
    give_b, keep_b = project(table, (own_b, *got_b), out_weight)
    return total(table, keep_b, lax.all_gather(give_b, "core"), across)


def solution(mesh):
    fine = Mesh(mesh.devices.reshape(4, 2, 8, 2, 2), ("x", "yl", "z", "yh", "core"))
    ctx, tp = ("x", "yl", "z"), ("yh", "core")
    return jax.shard_map(
        on_device,
        mesh=fine,
        in_specs=(P(ctx, tp),) * 5 + (P(), P(), P(tp, None)),
        out_specs=P((*ctx, *tp), None),
        check_vma=False,
    )
```

```python
import functools

import jax
import jax.numpy as jnp
from jax import lax
from jax.experimental import pallas as pl
from jax.experimental.pallas import tpu as pltpu
from jax.sharding import Mesh, PartitionSpec as P

HEADS = 8
D = 128
BLK = 96
TOK = 2 * BLK
CACHE = 64
SHARD = 2 * (TOK + CACHE)
ROWS = HEADS * BLK
TILE = 512
NEG = -1e30
SCALE = D**-0.5 * 1.4426950408889634
PLACE = 128
OUT_ROWS = D + 16
NT = (((1,), (1,)), ((), ()))
TN = (((0,), (0,)), ((), ()))
VMEM = pltpu.VMEM


def attend_chunk(work, sets, steps, first, last, *refs):
    refs = list(refs)

    def take(count):
        taken = refs[:count]
        del refs[:count]
        return taken

    n_query = len(work)
    (table_ref,) = take(1)
    q_refs = take(len(sets))
    msgs = take(len(steps))
    old = [] if first else take(3 * n_query)
    outs = take(n_query if last else 3 * n_query)
    m_all, l_all, acc_all, qx, kx, vx, s_a, s_b, ends, marks, item_block, item_tile = refs
    x, yl, z, offset, yh = (table_ref[PLACE + i] for i in (0, 1, 2, 3, 5))
    n_keys = 256 * 2 * len(steps)

    token = lax.broadcasted_iota(jnp.int32, (BLK, D), 0)
    column = lax.broadcasted_iota(jnp.int32, (BLK, D), 1)
    hidden = ((column < BLK) & (column > token)) | (column == BLK)
    q_extra = jnp.where(hidden, NEG, 0.0).astype(jnp.bfloat16)
    own_rows = jnp.where(column == token, 1.0, 0.0).astype(jnp.bfloat16)
    half_of = [yh if role else 1 - yh for _, role in work]
    for qb, (g, role) in enumerate(work):
        src = q_refs[sets.index(g)]
        at = pl.ds(pl.multiple_of(half_of[qb] * BLK, 32), BLK)
        for h in range(HEADS):
            rows = slice(h * BLK, (h + 1) * BLK)
            qx[qb, rows, :D] = src[at, h * D : (h + 1) * D]
            qx[qb, rows, D:] = q_extra
    kx[:, D:] = jnp.zeros((kx.shape[0], D), jnp.bfloat16)
    kx[n_keys - 512 :, :D] = jnp.zeros((kx.shape[0] - n_keys + 512, D), jnp.bfloat16)
    vx[...] = jnp.zeros_like(vx)

    ctxs = []
    for step in steps:
        zz = lax.rem(z + step + 8, 8)
        ctxs += [x * 16 + yl * 8 + zz, (3 - x) * 16 + yl * 8 + zz]
    cache_rows = jnp.int32(0)
    slot = lax.broadcasted_iota(jnp.int32, (CACHE, D), 0)
    lane = lax.broadcasted_iota(jnp.int32, (CACHE, D), 1)
    for j, ctx in enumerate(ctxs):
        filled = offset - ctx * CACHE
        src = msgs[j // 2]
        base = (j % 2) * SHARD

        @pl.when(filled > 0)
        def _(src=src, base=base, at=cache_rows, filled=filled):
            to = pl.ds(pl.multiple_of(at, CACHE), CACHE)
            kx[to, :D] = src[base + TOK : base + TOK + CACHE, :]
            kx[to, D:] = jnp.where((slot >= filled) & (lane == BLK), 1.0, 0.0).astype(jnp.bfloat16)
            vx[to, :] = src[base + 2 * TOK + CACHE : base + SHARD, :]

        cache_rows = cache_rows + jnp.where(filled > 0, CACHE, 0)

    ids = [table_ref[2 * ctx + b] for ctx in ctxs for b in range(2)]
    for j, mine in enumerate(ids):
        rank = jnp.int32(0)
        for k, other in enumerate(ids):
            if k != j:
                rank = rank + (other < mine).astype(jnp.int32)
        to = pl.ds(pl.multiple_of(cache_rows + rank * BLK, 32), BLK)
        src = msgs[j // 4]
        base = ((j // 2) % 2) * SHARD + (j % 2) * BLK
        kx[to, :D] = src[base : base + BLK, :]
        vx[to, :] = src[base + TOK + CACHE : base + TOK + CACHE + BLK, :]

    items = jnp.int32(0)
    for qb, (g, role) in enumerate(work):
        gx, gy = g % 2, g // 2
        q_x = x + 1 - 2 * lax.rem(x, 2) if gx else x
        q_y = 1 - yl if gy else yl
        q_id = table_ref[2 * (q_x * 16 + q_y * 8 + z) + half_of[qb]]
        count = jnp.int32(0)
        own = jnp.int32(0)
        for k in ids:
            count = count + (k <= q_id).astype(jnp.int32)
            own = own + (k == q_id).astype(jnp.int32)
        end = cache_rows + count * BLK
        ends[qb] = end
        marks[qb] = jnp.where(own > 0, end - BLK, n_keys + TILE)
        tiles = (end + TILE - 1) // TILE

        def add(t, at, qb=qb):
            item_block[at] = qb
            item_tile[at] = t
            return at + 1

        items = lax.fori_loop(0, tiles, add, items)
        if first:
            m_all[qb] = jnp.full((8, ROWS), NEG, jnp.float32)
            l_all[qb] = jnp.zeros((8, ROWS), jnp.float32)
            acc_all[qb] = jnp.zeros((D, ROWS), jnp.float32)
        else:
            m_all[qb], l_all[qb], acc_all[qb] = (ref[...] for ref in old[3 * qb : 3 * qb + 3])

    pad_lane = lax.broadcasted_iota(jnp.int32, (TILE, D), 1)
    pad_rows = jnp.where(pad_lane == BLK, 1.0, 0.0).astype(jnp.bfloat16)

    def scores(k, before):
        old, new = item_block[before], item_block[k]
        kx[pl.ds(pl.multiple_of(ends[old], 32), TILE), D:] = jnp.zeros_like(pad_rows)
        kx[pl.ds(pl.multiple_of(marks[old], 32), BLK), D:] = jnp.zeros_like(own_rows)
        kx[pl.ds(pl.multiple_of(ends[new], 32), TILE), D:] = pad_rows
        kx[pl.ds(pl.multiple_of(marks[new], 32), BLK), D:] = own_rows
        keys = kx[pl.ds(pl.multiple_of(item_tile[k] * TILE, TILE), TILE), :]
        return lax.dot_general(keys, qx[new], NT, preferred_element_type=jnp.float32)

    def absorb(s_ref, k):
        qb = item_block[k]
        s = s_ref[...]
        m0 = m_all[qb]
        m1 = jnp.maximum(m0, jnp.max(s, axis=0, keepdims=True) * SCALE)
        factor = jnp.exp2(m0 - m1)
        p = jnp.exp2(s * SCALE - m1[:1])
        l_all[qb] = l_all[qb] * factor + jnp.sum(p, axis=0, keepdims=True)
        m_all[qb] = m1
        values = vx[pl.ds(pl.multiple_of(item_tile[k] * TILE, TILE), TILE), :]
        acc_all[qb] = acc_all[qb] * factor[:1] + lax.dot_general(
            values, p.astype(jnp.bfloat16), TN, preferred_element_type=jnp.float32
        )

    @pl.when(items > 0)
    def _():
        s_a[...] = scores(0, 0)

        def pair(j, c):
            k = 2 * j
            s_b[...] = scores(k + 1, k)
            absorb(s_a, k)
            s_a[...] = scores(k + 2, k + 1)
            absorb(s_b, k + 1)
            return c

        lax.fori_loop(0, (items - 1) // 2, pair, 0)

        @pl.when(items % 2 == 0)
        def _():
            s_b[...] = scores(items - 1, items - 2)
            absorb(s_a, items - 2)
            absorb(s_b, items - 1)

        @pl.when(items % 2 == 1)
        def _():
            absorb(s_a, items - 1)

    for qb in range(n_query):
        if last:
            total = l_all[qb]
            some = total > 0.0
            safe = jnp.where(some, total, 1.0)
            logsum = jnp.where(some, m_all[qb] + jnp.log2(safe), NEG)
            high = logsum.astype(jnp.bfloat16)
            rest = logsum - high.astype(jnp.float32)
            mid = rest.astype(jnp.bfloat16)
            low = (rest - mid.astype(jnp.float32)).astype(jnp.bfloat16)
            row = lax.broadcasted_iota(jnp.int32, (16, ROWS), 0)
            h2, m2, l2 = (jnp.concatenate([v, v], 0).astype(jnp.float32) for v in (high, mid, low))
            outs[qb][:D, :] = (acc_all[qb] / safe[:1]).astype(jnp.bfloat16)
            outs[qb][D:, :] = jnp.where(row == 0, h2, jnp.where(row == 1, m2, l2)).astype(jnp.bfloat16)
        else:
            for ref, kept in zip(outs[3 * qb : 3 * qb + 3], (m_all, l_all, acc_all)):
                ref[...] = kept[qb]


def run_chunk(work, steps, state, last, table, queries, messages):
    first = work[0] not in state
    sets = sorted({g for g, _ in work})
    n_query = len(work)
    n_keys = 256 * 2 * len(steps)
    keep = n_keys + TILE + 128
    max_items = n_query * (n_keys // TILE + 1) + 2
    shapes = [(8, ROWS), (8, ROWS), (D, ROWS)]
    smem = pl.BlockSpec(memory_space=pltpu.SMEM)
    vmem = pl.BlockSpec(memory_space=VMEM)
    operands = [table, *(queries[g] for g in sets), *messages]
    if not first:
        operands += [array for key in work for array in state[key]]
    if last:
        out_shape = [jax.ShapeDtypeStruct((OUT_ROWS, ROWS), jnp.bfloat16)] * n_query
    else:
        out_shape = [jax.ShapeDtypeStruct(s, jnp.float32) for s in shapes] * n_query
    pairs = n_query * n_keys * ROWS * 6 // 10
    name = "_".join(["attend", *(str(g) + "AB"[role] for g, role in work), str(len(steps))])
    results = pl.pallas_call(
        functools.partial(attend_chunk, tuple(work), tuple(sets), tuple(steps), first, last),
        out_shape=out_shape,
        in_specs=[smem] + [vmem] * (len(operands) - 1),
        out_specs=[vmem] * len(out_shape),
        scratch_shapes=[VMEM((n_query, *s), jnp.float32) for s in shapes]
        + [
            VMEM((n_query, ROWS, 2 * D), jnp.bfloat16),
            VMEM((keep, 2 * D), jnp.bfloat16),
            VMEM((keep, D), jnp.bfloat16),
            VMEM((TILE, ROWS), jnp.float32),
            VMEM((TILE, ROWS), jnp.float32),
            pltpu.SMEM((8,), jnp.int32),
            pltpu.SMEM((8,), jnp.int32),
            pltpu.SMEM((max_items,), jnp.int32),
            pltpu.SMEM((max_items,), jnp.int32),
        ],
        compiler_params=pltpu.CompilerParams(vmem_limit_bytes=24 * 2**20),
        cost_estimate=pl.CostEstimate(flops=pairs * 1024, bytes_accessed=8 * 2**20, transcendentals=pairs),
        name=name,
    )(*operands)
    if last:
        return results
    for i, key in enumerate(work):
        state[key] = tuple(results[3 * i : 3 * i + 3])
    return state


def project_body(table_ref, a_ref, b_ref, c_ref, d_ref, w_ref, give_ref, mine_ref, att):
    parts = (a_ref, b_ref, c_ref, d_ref)
    logs = []
    for part in parts:
        row = part[D:, :].astype(jnp.float32)
        logs.append(row[0:1] + row[1:2] + row[2:3])
    top = functools.reduce(jnp.maximum, logs)
    weights = [jnp.exp2(v - top) for v in logs]
    share = 1.0 / sum(weights)
    mixed = sum(part[:D, :].astype(jnp.float32) * (w * share) for part, w in zip(parts, weights))
    turned = mixed.T.astype(jnp.bfloat16)
    for h in range(HEADS):
        att[:, h * D : (h + 1) * D] = turned[h * BLK : (h + 1) * BLK, :]
    core = table_ref[PLACE + 4]
    half = BLK // 2
    wide = 512
    for c in range(w_ref.shape[1] // wide):
        cols = slice(c * wide, (c + 1) * wide)
        full = jnp.dot(att[...], w_ref[:, cols], preferred_element_type=jnp.float32)
        give_ref[:, cols] = jnp.where(core == 0, full[half:], full[:half]).astype(jnp.bfloat16)
        mine_ref[:, cols] = jnp.where(core == 0, full[:half], full[half:])


def project(table, parts, weight):
    vmem = pl.BlockSpec(memory_space=VMEM)
    wide = weight.shape[1]
    return pl.pallas_call(
        project_body,
        out_shape=(
            jax.ShapeDtypeStruct((BLK // 2, wide), jnp.bfloat16),
            jax.ShapeDtypeStruct((BLK // 2, wide), jnp.float32),
        ),
        in_specs=[pl.BlockSpec(memory_space=pltpu.SMEM)] + [vmem] * 5,
        out_specs=(vmem, vmem),
        scratch_shapes=[VMEM((BLK, HEADS * D), jnp.bfloat16)],
        compiler_params=pltpu.CompilerParams(vmem_limit_bytes=24 * 2**20),
        cost_estimate=pl.CostEstimate(flops=2 * BLK * HEADS * D * wide, bytes_accessed=12 * 2**20, transcendentals=0),
        name="project",
    )(table, *parts, weight)


def total_body(a_ref, b_ref, out):
    out[...] = (a_ref[...].astype(jnp.float32) + b_ref[...].astype(jnp.float32)).astype(out.dtype)


def total(a, b, dtype):
    vmem = pl.BlockSpec(memory_space=VMEM)
    return pl.pallas_call(
        total_body,
        out_shape=jax.ShapeDtypeStruct(a.shape, dtype),
        in_specs=[vmem] * 2,
        out_specs=vmem,
        compiler_params=pltpu.CompilerParams(vmem_limit_bytes=8 * 2**20),
        name="total",
    )(a, b)


def stage_body(src, dst):
    dst[...] = src[...]


def stage(array):
    vmem = pl.BlockSpec(memory_space=VMEM)
    return pl.pallas_call(
        stage_body,
        out_shape=jax.ShapeDtypeStruct(array.shape, array.dtype),
        in_specs=[vmem],
        out_specs=vmem,
        compiler_params=pltpu.CompilerParams(vmem_limit_bytes=8 * 2**20),
        name="stage",
    )(array)


def on_device(queries, window_keys, window_values, stored_keys, stored_values, block_order, window_offset, out_weight):
    x, yl, z = lax.axis_index("x"), lax.axis_index("yl"), lax.axis_index("z")
    core, yh = lax.axis_index("core"), lax.axis_index("yh")
    place = jnp.stack([x, yl, z, window_offset[0], core, yh]).astype(jnp.int32)
    table = jnp.concatenate([block_order, place])
    shard = jnp.concatenate([window_keys, stored_keys, window_values, stored_values], 0)

    def along(array, axis, size, to):
        return lax.ppermute(array, axis, [(i, to(i)) for i in range(size)])

    shard, queries = lax.optimization_barrier((shard, queries))
    other = along(shard, "x", 4, lambda i: 3 - i)
    base = jnp.concatenate([shard, other], 0)
    pair = [(a, b) for a in range(4) for b in range(2)]
    both = [(2 * a + b, 2 * (a ^ 1) + (1 - b)) for a, b in pair]
    to_member = [
        lambda v: v,
        lambda v: along(v, "x", 4, lambda i: i ^ 1),
        lambda v: along(v, "yl", 2, lambda i: 1 - i),
        lambda v: lax.ppermute(v, ("x", "yl"), both),
    ]
    q_sets = [queries] + [to_member[g](queries) for g in (1, 2, 3)]
    up = lambda a: along(a, "z", 8, lambda i: (i + 1) % 8)
    down = lambda a: along(a, "z", 8, lambda i: (i - 1) % 8)
    base, table, q_sets[0] = lax.optimization_barrier((base, table, stage(queries)))
    a1, b1 = up(base), down(base)
    a2, b2 = up(a1), down(b1)
    state = {}
    run = lambda work, steps, messages, last=False: run_chunk(work, steps, state, last, table, q_sets, messages)
    tie = lax.optimization_barrier
    near = (0, -1, 1), (base, a1, b1)
    A, B = 0, 1
    run([(0, A), (0, B)], *near)
    run([(3, A), (3, B)], *near)
    a2, b2, state[0, A], state[3, A] = tie((a2, b2, state[0, A], state[3, A]))
    a3, b3 = up(a2), down(b2)
    far = jnp.concatenate([up(a3[:SHARD]), down(b3[SHARD:])], 0)
    run([(1, A), (1, B), (2, A), (2, B)], *near)
    run([(g, r) for r in (A, B) for g in (1, 2, 3)], (-2, 2), (a2, b2))
    end = (-3, 3, 4), (a3, b3, far)
    sent_a = run([(3, A), (1, A), (2, A)], *end, True)
    *sent_a, state[3, B] = tie((*sent_a, state[3, B]))
    got_a = [to_member[g](v) for g, v in zip((3, 1, 2), sent_a)]
    sent_b = run([(3, B), (1, B), (2, B)], *end, True)
    got_b = [to_member[g](v) for g, v in zip((3, 1, 2), sent_b)]
    *got_a, state[0, A] = tie((*got_a, state[0, A]))
    own_a, own_b = run([(0, A), (0, B)], (-2, 2, -3, 3, 4), (a2, b2, a3, b3, far), True)
    swap = lambda v, axis: along(v, axis, 2, lambda i: 1 - i)
    give_a, keep_a = project(table, (own_a, *got_a), out_weight)
    give_a, *got_b = tie((give_a, *got_b))
    across = swap(total(keep_a, swap(give_a, "core"), jnp.bfloat16), "yh")
    give_b, keep_b = project(table, (own_b, *got_b), out_weight)
    return total(total(keep_b, across, jnp.float32), swap(give_b, "core"), jnp.bfloat16)


def solution(mesh):
    fine = Mesh(mesh.devices.reshape(4, 2, 8, 2, 2), ("x", "yl", "z", "yh", "core"))
    ctx, tp = ("x", "yl", "z"), ("yh", "core")
    return jax.shard_map(
        on_device,
        mesh=fine,
        in_specs=(P(ctx, tp),) * 5 + (P(), P(), P(tp, None)),
        out_specs=P((*ctx, *tp), None),
        check_vma=False,
    )
```

```python
import functools

import jax
import jax.numpy as jnp
from jax import lax
from jax.experimental import pallas as pl
from jax.experimental.pallas import tpu as pltpu
from jax.sharding import Mesh, PartitionSpec as P

HEADS = 8
D = 128
BLK = 96
TOK = 2 * BLK
CACHE = 64
SHARD = 2 * (TOK + CACHE)
ROWS = HEADS * BLK
TILE = 384
NEG = -1e30
SCALE = D**-0.5 * 1.4426950408889634
PLACE = 128
OUT_ROWS = D + 16
NT = (((1,), (1,)), ((), ()))
TN = (((0,), (0,)), ((), ()))
VMEM = pltpu.VMEM


def attend_chunk(work, sets, steps, first, last, *refs):
    refs = list(refs)

    def take(count):
        taken = refs[:count]
        del refs[:count]
        return taken

    n_query = len(work)
    (table_ref,) = take(1)
    q_refs = take(len(sets))
    msgs = take(len(steps))
    old = [] if first else take(3 * n_query)
    outs = take(n_query if last else 3 * n_query)
    m_all, l_all, acc_all, qx, kx, vx, s_a, s_b, ends, marks, item_block, item_tile = refs
    x, yl, z, offset, yh = (table_ref[PLACE + i] for i in (0, 1, 2, 3, 5))
    n_keys = 256 * 2 * len(steps)

    token = lax.broadcasted_iota(jnp.int32, (BLK, D), 0)
    column = lax.broadcasted_iota(jnp.int32, (BLK, D), 1)
    hidden = ((column < BLK) & (column > token)) | (column == BLK)
    q_extra = jnp.where(hidden, NEG, 0.0).astype(jnp.bfloat16)
    own_rows = jnp.where(column == token, 1.0, 0.0).astype(jnp.bfloat16)
    half_of = [yh if role else 1 - yh for _, role in work]
    for qb, (g, role) in enumerate(work):
        src = q_refs[sets.index(g)]
        at = pl.ds(pl.multiple_of(half_of[qb] * BLK, 32), BLK)
        for h in range(HEADS):
            rows = slice(h * BLK, (h + 1) * BLK)
            qx[qb, rows, :D] = src[at, h * D : (h + 1) * D]
            qx[qb, rows, D:] = q_extra
    kx[:, D:] = jnp.zeros((kx.shape[0], D), jnp.bfloat16)
    sure = n_keys - 2 * CACHE * len(steps)
    kx[sure:, :D] = jnp.zeros((kx.shape[0] - sure, D), jnp.bfloat16)
    vx[...] = jnp.zeros_like(vx)

    ctxs = []
    for step in steps:
        zz = lax.rem(z + step + 8, 8)
        ctxs += [x * 16 + yl * 8 + zz, (3 - x) * 16 + yl * 8 + zz]
    cache_rows = jnp.int32(0)
    slot = lax.broadcasted_iota(jnp.int32, (CACHE, D), 0)
    lane = lax.broadcasted_iota(jnp.int32, (CACHE, D), 1)
    for j, ctx in enumerate(ctxs):
        filled = offset - ctx * CACHE
        src = msgs[j // 2]
        base = (j % 2) * SHARD

        @pl.when(filled > 0)
        def _(src=src, base=base, at=cache_rows, filled=filled):
            to = pl.ds(pl.multiple_of(at, CACHE), CACHE)
            kx[to, :D] = src[base + TOK : base + TOK + CACHE, :]
            kx[to, D:] = jnp.where((slot >= filled) & (lane == BLK), 1.0, 0.0).astype(jnp.bfloat16)
            vx[to, :] = src[base + 2 * TOK + CACHE : base + SHARD, :]

        cache_rows = cache_rows + jnp.where(filled > 0, CACHE, 0)

    ids = [table_ref[2 * ctx + b] for ctx in ctxs for b in range(2)]
    for j, mine in enumerate(ids):
        rank = jnp.int32(0)
        for k, other in enumerate(ids):
            if k != j:
                rank = rank + (other < mine).astype(jnp.int32)
        to = pl.ds(pl.multiple_of(cache_rows + rank * BLK, 32), BLK)
        src = msgs[j // 4]
        base = ((j // 2) % 2) * SHARD + (j % 2) * BLK
        kx[to, :D] = src[base : base + BLK, :]
        vx[to, :] = src[base + TOK + CACHE : base + TOK + CACHE + BLK, :]

    items = jnp.int32(0)
    for qb, (g, role) in enumerate(work):
        gx, gy = g % 2, g // 2
        q_x = x + 1 - 2 * lax.rem(x, 2) if gx else x
        q_y = 1 - yl if gy else yl
        q_id = table_ref[2 * (q_x * 16 + q_y * 8 + z) + half_of[qb]]
        count = jnp.int32(0)
        own = jnp.int32(0)
        for k in ids:
            count = count + (k <= q_id).astype(jnp.int32)
            own = own + (k == q_id).astype(jnp.int32)
        end = cache_rows + count * BLK
        ends[qb] = end
        marks[qb] = jnp.where(own > 0, end - BLK, n_keys + TILE)
        tiles = (end + TILE - 1) // TILE

        def add(t, at, qb=qb):
            item_block[at] = qb
            item_tile[at] = t
            return at + 1

        items = lax.fori_loop(0, tiles, add, items)
        if first:
            m_all[qb] = jnp.full((8, ROWS), NEG, jnp.float32)
            l_all[qb] = jnp.zeros((8, ROWS), jnp.float32)
            acc_all[qb] = jnp.zeros((D, ROWS), jnp.float32)
        else:
            m_all[qb], l_all[qb], acc_all[qb] = (ref[...] for ref in old[3 * qb : 3 * qb + 3])

    pad_lane = lax.broadcasted_iota(jnp.int32, (TILE, D), 1)
    pad_rows = jnp.where(pad_lane == BLK, 1.0, 0.0).astype(jnp.bfloat16)

    def scores(k, before):
        old, new = item_block[before], item_block[k]
        kx[pl.ds(pl.multiple_of(ends[old], 32), TILE), D:] = jnp.zeros_like(pad_rows)
        kx[pl.ds(pl.multiple_of(marks[old], 32), BLK), D:] = jnp.zeros_like(own_rows)
        kx[pl.ds(pl.multiple_of(ends[new], 32), TILE), D:] = pad_rows
        kx[pl.ds(pl.multiple_of(marks[new], 32), BLK), D:] = own_rows
        keys = kx[pl.ds(pl.multiple_of(item_tile[k] * TILE, TILE), TILE), :]
        return lax.dot_general(keys, qx[new], NT, preferred_element_type=jnp.float32)

    def absorb(s_ref, k):
        qb = item_block[k]
        s = s_ref[...]
        m0 = m_all[qb]
        m1 = jnp.maximum(m0, jnp.max(s, axis=0, keepdims=True) * SCALE)
        factor = jnp.exp2(m0 - m1)
        p = jnp.exp2(s * SCALE - m1[:1])
        l_all[qb] = l_all[qb] * factor + jnp.sum(p, axis=0, keepdims=True)
        m_all[qb] = m1
        values = vx[pl.ds(pl.multiple_of(item_tile[k] * TILE, TILE), TILE), :]
        acc_all[qb] = acc_all[qb] * factor[:1] + lax.dot_general(
            values, p.astype(jnp.bfloat16), TN, preferred_element_type=jnp.float32
        )

    @pl.when(items > 0)
    def _():
        s_a[...] = scores(0, 0)

        def pair(j, c):
            k = 2 * j
            s_b[...] = scores(k + 1, k)
            absorb(s_a, k)
            s_a[...] = scores(k + 2, k + 1)
            absorb(s_b, k + 1)
            return c

        lax.fori_loop(0, (items - 1) // 2, pair, 0)

        @pl.when(items % 2 == 0)
        def _():
            s_b[...] = scores(items - 1, items - 2)
            absorb(s_a, items - 2)
            absorb(s_b, items - 1)

        @pl.when(items % 2 == 1)
        def _():
            absorb(s_a, items - 1)

    for qb in range(n_query):
        if last:
            total = l_all[qb]
            some = total > 0.0
            safe = jnp.where(some, total, 1.0)
            logsum = jnp.where(some, m_all[qb] + jnp.log2(safe), NEG)
            high = logsum.astype(jnp.bfloat16)
            rest = logsum - high.astype(jnp.float32)
            mid = rest.astype(jnp.bfloat16)
            low = (rest - mid.astype(jnp.float32)).astype(jnp.bfloat16)
            row = lax.broadcasted_iota(jnp.int32, (16, ROWS), 0)
            h2, m2, l2 = (jnp.concatenate([v, v], 0).astype(jnp.float32) for v in (high, mid, low))
            outs[qb][:D, :] = (acc_all[qb] / safe[:1]).astype(jnp.bfloat16)
            outs[qb][D:, :] = jnp.where(row == 0, h2, jnp.where(row == 1, m2, l2)).astype(jnp.bfloat16)
        else:
            for ref, kept in zip(outs[3 * qb : 3 * qb + 3], (m_all, l_all, acc_all)):
                ref[...] = kept[qb]


def run_chunk(work, steps, state, last, table, queries, messages):
    first = work[0] not in state
    sets = sorted({g for g, _ in work})
    n_query = len(work)
    n_keys = 256 * 2 * len(steps)
    keep = n_keys + TILE + 128
    max_items = n_query * (n_keys // TILE + 1) + 2
    shapes = [(8, ROWS), (8, ROWS), (D, ROWS)]
    smem = pl.BlockSpec(memory_space=pltpu.SMEM)
    vmem = pl.BlockSpec(memory_space=VMEM)
    operands = [table, *(queries[g] for g in sets), *messages]
    if not first:
        operands += [array for key in work for array in state[key]]
    if last:
        out_shape = [jax.ShapeDtypeStruct((OUT_ROWS, ROWS), jnp.bfloat16)] * n_query
    else:
        out_shape = [jax.ShapeDtypeStruct(s, jnp.float32) for s in shapes] * n_query
    pairs = n_query * n_keys * ROWS * 6 // 10
    name = "_".join(["attend", *(str(g) + "AB"[role] for g, role in work), str(len(steps))])
    results = pl.pallas_call(
        functools.partial(attend_chunk, tuple(work), tuple(sets), tuple(steps), first, last),
        out_shape=out_shape,
        in_specs=[smem] + [vmem] * (len(operands) - 1),
        out_specs=[vmem] * len(out_shape),
        scratch_shapes=[VMEM((n_query, *s), jnp.float32) for s in shapes]
        + [
            VMEM((n_query, ROWS, 2 * D), jnp.bfloat16),
            VMEM((keep, 2 * D), jnp.bfloat16),
            VMEM((keep, D), jnp.bfloat16),
            VMEM((TILE, ROWS), jnp.float32),
            VMEM((TILE, ROWS), jnp.float32),
            pltpu.SMEM((8,), jnp.int32),
            pltpu.SMEM((8,), jnp.int32),
            pltpu.SMEM((max_items,), jnp.int32),
            pltpu.SMEM((max_items,), jnp.int32),
        ],
        compiler_params=pltpu.CompilerParams(vmem_limit_bytes=24 * 2**20),
        cost_estimate=pl.CostEstimate(flops=pairs * 1024, bytes_accessed=8 * 2**20, transcendentals=pairs),
        name=name,
    )(*operands)
    if last:
        return results
    for i, key in enumerate(work):
        state[key] = tuple(results[3 * i : 3 * i + 3])
    return state


def project_body(table_ref, a_ref, b_ref, c_ref, d_ref, w_ref, give_ref, mine_ref, att):
    parts = (a_ref, b_ref, c_ref, d_ref)
    logs = []
    for part in parts:
        row = part[D:, :].astype(jnp.float32)
        logs.append(row[0:1] + row[1:2] + row[2:3])
    top = functools.reduce(jnp.maximum, logs)
    weights = [jnp.exp2(v - top) for v in logs]
    share = 1.0 / sum(weights)
    mixed = sum(part[:D, :].astype(jnp.float32) * (w * share) for part, w in zip(parts, weights))
    turned = mixed.T.astype(jnp.bfloat16)
    for h in range(HEADS):
        att[:, h * D : (h + 1) * D] = turned[h * BLK : (h + 1) * BLK, :]
    core = table_ref[PLACE + 4]
    half = BLK // 2
    wide = 512
    for c in range(w_ref.shape[1] // wide):
        cols = slice(c * wide, (c + 1) * wide)
        full = jnp.dot(att[...], w_ref[:, cols], preferred_element_type=jnp.float32)
        give_ref[:, cols] = jnp.where(core == 0, full[half:], full[:half]).astype(jnp.bfloat16)
        mine_ref[:, cols] = jnp.where(core == 0, full[:half], full[half:])


def project(table, parts, weight):
    vmem = pl.BlockSpec(memory_space=VMEM)
    wide = weight.shape[1]
    return pl.pallas_call(
        project_body,
        out_shape=(
            jax.ShapeDtypeStruct((BLK // 2, wide), jnp.bfloat16),
            jax.ShapeDtypeStruct((BLK // 2, wide), jnp.float32),
        ),
        in_specs=[pl.BlockSpec(memory_space=pltpu.SMEM)] + [vmem] * 5,
        out_specs=(vmem, vmem),
        scratch_shapes=[VMEM((BLK, HEADS * D), jnp.bfloat16)],
        compiler_params=pltpu.CompilerParams(vmem_limit_bytes=24 * 2**20),
        cost_estimate=pl.CostEstimate(flops=2 * BLK * HEADS * D * wide, bytes_accessed=12 * 2**20, transcendentals=0),
        name="project",
    )(table, *parts, weight)


def total_body(a_ref, b_ref, out):
    out[...] = (a_ref[...].astype(jnp.float32) + b_ref[...].astype(jnp.float32)).astype(out.dtype)


def total(a, b, dtype):
    vmem = pl.BlockSpec(memory_space=VMEM)
    return pl.pallas_call(
        total_body,
        out_shape=jax.ShapeDtypeStruct(a.shape, dtype),
        in_specs=[vmem] * 2,
        out_specs=vmem,
        compiler_params=pltpu.CompilerParams(vmem_limit_bytes=8 * 2**20),
        name="total",
    )(a, b)


def stage_body(src, dst):
    dst[...] = src[...]


def stage(array):
    vmem = pl.BlockSpec(memory_space=VMEM)
    return pl.pallas_call(
        stage_body,
        out_shape=jax.ShapeDtypeStruct(array.shape, array.dtype),
        in_specs=[vmem],
        out_specs=vmem,
        compiler_params=pltpu.CompilerParams(vmem_limit_bytes=8 * 2**20),
        name="stage",
    )(array)


def on_device(queries, window_keys, window_values, stored_keys, stored_values, block_order, window_offset, out_weight):
    x, yl, z = lax.axis_index("x"), lax.axis_index("yl"), lax.axis_index("z")
    core, yh = lax.axis_index("core"), lax.axis_index("yh")
    place = jnp.stack([x, yl, z, window_offset[0], core, yh]).astype(jnp.int32)
    table = jnp.concatenate([block_order, place])
    shard = jnp.concatenate([window_keys, stored_keys, window_values, stored_values], 0)

    def along(array, axis, size, to):
        return lax.ppermute(array, axis, [(i, to(i)) for i in range(size)])

    shard, queries = lax.optimization_barrier((shard, queries))
    other = along(shard, "x", 4, lambda i: 3 - i)
    base = jnp.concatenate([shard, other], 0)
    pair = [(a, b) for a in range(4) for b in range(2)]
    both = [(2 * a + b, 2 * (a ^ 1) + (1 - b)) for a, b in pair]
    to_member = [
        lambda v: v,
        lambda v: along(v, "x", 4, lambda i: i ^ 1),
        lambda v: along(v, "yl", 2, lambda i: 1 - i),
        lambda v: lax.ppermute(v, ("x", "yl"), both),
    ]
    q_sets = [queries] + [to_member[g](queries) for g in (1, 2, 3)]
    up = lambda a: along(a, "z", 8, lambda i: (i + 1) % 8)
    down = lambda a: along(a, "z", 8, lambda i: (i - 1) % 8)
    base, table, q_sets[0] = lax.optimization_barrier((base, table, stage(queries)))
    a1, b1 = up(base), down(base)
    a2, b2 = up(a1), down(b1)
    state = {}
    run = lambda work, steps, messages, last=False: run_chunk(work, steps, state, last, table, q_sets, messages)
    tie = lax.optimization_barrier
    near = (0, -1, 1), (base, a1, b1)
    A, B = 0, 1
    run([(0, A), (0, B)], *near)
    run([(3, A), (3, B)], *near)
    a2, b2, state[0, A], state[3, A] = tie((a2, b2, state[0, A], state[3, A]))
    a3, b3 = up(a2), down(b2)
    far = jnp.concatenate([up(a3[:SHARD]), down(b3[SHARD:])], 0)
    run([(1, A), (1, B), (2, A), (2, B)], *near)
    run([(g, r) for r in (A, B) for g in (1, 2, 3)], (-2, 2), (a2, b2))
    end = (-3, 3, 4), (a3, b3, far)
    sent_a = run([(3, A), (1, A), (2, A)], *end, True)
    *sent_a, state[3, B] = tie((*sent_a, state[3, B]))
    got_a = [to_member[g](v) for g, v in zip((3, 1, 2), sent_a)]
    sent_b = run([(3, B), (1, B), (2, B)], *end, True)
    got_b = [to_member[g](v) for g, v in zip((3, 1, 2), sent_b)]
    *got_a, state[0, A] = tie((*got_a, state[0, A]))
    rest = (-2, 2, -3, 3, 4), (a2, b2, a3, b3, far)
    (own_a,) = run([(0, A)], *rest, True)
    swap = lambda v, axis: along(v, axis, 2, lambda i: 1 - i)
    give_a, keep_a = project(table, (own_a, *got_a), out_weight)
    give_a, *got_b = tie((give_a, *got_b))
    sum_a = total(keep_a, swap(give_a, "core"), jnp.bfloat16)
    sum_a, state[0, B] = tie((sum_a, state[0, B]))
    across = swap(sum_a, "yh")
    (own_b,) = run([(0, B)], *rest, True)
    give_b, keep_b = project(table, (own_b, *got_b), out_weight)
    keep_b = total(keep_b, across, jnp.float32)
    return (keep_b + swap(give_b, "core").astype(jnp.float32)).astype(jnp.bfloat16)


def solution(mesh):
    fine = Mesh(mesh.devices.reshape(4, 2, 8, 2, 2), ("x", "yl", "z", "yh", "core"))
    ctx, tp = ("x", "yl", "z"), ("yh", "core")
    return jax.shard_map(
        on_device,
        mesh=fine,
        in_specs=(P(ctx, tp),) * 5 + (P(), P(), P(tp, None)),
        out_specs=P((*ctx, *tp), None),
        check_vma=False,
    )
```

```python
import functools

import jax
import jax.numpy as jnp
from jax import lax
from jax.experimental import pallas as pl
from jax.experimental.pallas import tpu as pltpu
from jax.sharding import Mesh, PartitionSpec as P

HEADS = 8
D = 128
BLK = 96
TOK = 2 * BLK
CACHE = 64
SHARD = 2 * (TOK + CACHE)
ROWS = HEADS * BLK
TILE = 256
NEG = -1e30
SCALE = D**-0.5 * 1.4426950408889634
PLACE = 128
OUT_ROWS = D + 16
NT = (((1,), (1,)), ((), ()))
TN = (((0,), (0,)), ((), ()))
VMEM = pltpu.VMEM


def attend_chunk(work, sets, steps, first, last, *refs):
    refs = list(refs)

    def take(count):
        taken = refs[:count]
        del refs[:count]
        return taken

    n_query = len(work)
    (table_ref,) = take(1)
    q_refs = take(len(sets))
    msgs = take(len(steps))
    old = [] if first else take(3 * n_query)
    outs = take(n_query if last else 3 * n_query)
    m_all, l_all, acc_all, qx, kx, vx, s_a, s_b, ends, marks, item_block, item_tile = refs
    x, yl, z, offset, yh = (table_ref[PLACE + i] for i in (0, 1, 2, 3, 5))
    n_keys = 256 * 2 * len(steps)

    token = lax.broadcasted_iota(jnp.int32, (BLK, D), 0)
    column = lax.broadcasted_iota(jnp.int32, (BLK, D), 1)
    hidden = ((column < BLK) & (column > token)) | (column == BLK)
    q_extra = jnp.where(hidden, NEG, 0.0).astype(jnp.bfloat16)
    own_rows = jnp.where(column == token, 1.0, 0.0).astype(jnp.bfloat16)
    half_of = [yh if role else 1 - yh for _, role in work]
    for qb, (g, role) in enumerate(work):
        src = q_refs[sets.index(g)]
        at = pl.ds(pl.multiple_of(half_of[qb] * BLK, 32), BLK)

        def stage_head(h, carry, qb=qb, src=src, at=at):
            rows = pl.ds(pl.multiple_of(h * BLK, 32), BLK)
            qx[qb, rows, :D] = src[at, pl.ds(pl.multiple_of(h * D, D), D)]
            qx[qb, rows, D:] = q_extra
            return carry

        lax.fori_loop(0, HEADS, stage_head, 0)

    def clear(i, carry):
        rows = pl.ds(pl.multiple_of(i * D, D), D)
        kx[rows, D:] = jnp.zeros((D, D), jnp.bfloat16)
        vx[rows, :] = jnp.zeros((D, D), jnp.bfloat16)
        return carry

    def clear_keys(i, carry):
        kx[pl.ds(pl.multiple_of(i * D, D), D), :D] = jnp.zeros((D, D), jnp.bfloat16)
        return carry

    lax.fori_loop(0, kx.shape[0] // D, clear, 0)
    lax.fori_loop(n_keys // D - len(steps), kx.shape[0] // D, clear_keys, 0)

    ctxs = []
    for step in steps:
        zz = lax.rem(z + step + 8, 8)
        ctxs += [x * 16 + yl * 8 + zz, (3 - x) * 16 + yl * 8 + zz]
    cache_rows = jnp.int32(0)
    slot = lax.broadcasted_iota(jnp.int32, (CACHE, D), 0)
    lane = lax.broadcasted_iota(jnp.int32, (CACHE, D), 1)
    for j, ctx in enumerate(ctxs):
        filled = offset - ctx * CACHE
        src = msgs[j // 2]
        base = (j % 2) * SHARD

        @pl.when(filled > 0)
        def _(src=src, base=base, at=cache_rows, filled=filled):
            to = pl.ds(pl.multiple_of(at, CACHE), CACHE)
            kx[to, :D] = src[base + TOK : base + TOK + CACHE, :]
            kx[to, D:] = jnp.where((slot >= filled) & (lane == BLK), 1.0, 0.0).astype(jnp.bfloat16)
            vx[to, :] = src[base + 2 * TOK + CACHE : base + SHARD, :]

        cache_rows = cache_rows + jnp.where(filled > 0, CACHE, 0)

    ids = [table_ref[2 * ctx + b] for ctx in ctxs for b in range(2)]
    for j, mine in enumerate(ids):
        rank = jnp.int32(0)
        for k, other in enumerate(ids):
            if k != j:
                rank = rank + (other < mine).astype(jnp.int32)
        to = pl.ds(pl.multiple_of(cache_rows + rank * BLK, 32), BLK)
        src = msgs[j // 4]
        base = ((j // 2) % 2) * SHARD + (j % 2) * BLK
        kx[to, :D] = src[base : base + BLK, :]
        vx[to, :] = src[base + TOK + CACHE : base + TOK + CACHE + BLK, :]

    items = jnp.int32(0)
    for qb, (g, role) in enumerate(work):
        gx, gy = g % 2, g // 2
        q_x = x + 1 - 2 * lax.rem(x, 2) if gx else x
        q_y = 1 - yl if gy else yl
        q_id = table_ref[2 * (q_x * 16 + q_y * 8 + z) + half_of[qb]]
        count = jnp.int32(0)
        own = jnp.int32(0)
        for k in ids:
            count = count + (k <= q_id).astype(jnp.int32)
            own = own + (k == q_id).astype(jnp.int32)
        end = cache_rows + count * BLK
        ends[qb] = end
        marks[qb] = jnp.where(own > 0, end - BLK, n_keys + TILE)
        tiles = (end + TILE - 1) // TILE

        def add(t, at, qb=qb):
            item_block[at] = qb
            item_tile[at] = t
            return at + 1

        items = lax.fori_loop(0, tiles, add, items)
        if first:
            m_all[qb] = jnp.full((8, ROWS), NEG, jnp.float32)
            l_all[qb] = jnp.zeros((8, ROWS), jnp.float32)
            acc_all[qb] = jnp.zeros((D, ROWS), jnp.float32)
        else:
            m_all[qb], l_all[qb] = old[3 * qb][...], old[3 * qb + 1][...]

            def bring(i, carry, qb=qb):
                rows = pl.ds(pl.multiple_of(i * 16, 16), 16)
                acc_all[qb, rows, :] = old[3 * qb + 2][rows, :]
                return carry

            lax.fori_loop(0, D // 16, bring, 0)

    pad_lane = lax.broadcasted_iota(jnp.int32, (TILE, D), 1)
    pad_rows = jnp.where(pad_lane == BLK, 1.0, 0.0).astype(jnp.bfloat16)

    def scores(k, before):
        old, new = item_block[before], item_block[k]
        kx[pl.ds(pl.multiple_of(ends[old], 32), TILE), D:] = jnp.zeros_like(pad_rows)
        kx[pl.ds(pl.multiple_of(marks[old], 32), BLK), D:] = jnp.zeros_like(own_rows)
        kx[pl.ds(pl.multiple_of(ends[new], 32), TILE), D:] = pad_rows
        kx[pl.ds(pl.multiple_of(marks[new], 32), BLK), D:] = own_rows
        keys = kx[pl.ds(pl.multiple_of(item_tile[k] * TILE, TILE), TILE), :]
        return lax.dot_general(keys, qx[new], NT, preferred_element_type=jnp.float32)

    def absorb(s_ref, k):
        qb = item_block[k]
        s = s_ref[...]
        m0 = m_all[qb]
        m1 = jnp.maximum(m0, jnp.max(s, axis=0, keepdims=True) * SCALE)
        factor = jnp.exp2(m0 - m1)
        p = jnp.exp2(s * SCALE - m1[:1])
        l_all[qb] = l_all[qb] * factor + jnp.sum(p, axis=0, keepdims=True)
        m_all[qb] = m1
        values = vx[pl.ds(pl.multiple_of(item_tile[k] * TILE, TILE), TILE), :]
        acc_all[qb] = acc_all[qb] * factor[:1] + lax.dot_general(
            values, p.astype(jnp.bfloat16), TN, preferred_element_type=jnp.float32
        )

    @pl.when(items > 0)
    def _():
        s_a[...] = scores(0, 0)

        def pair(j, c):
            k = 2 * j
            s_b[...] = scores(k + 1, k)
            absorb(s_a, k)
            s_a[...] = scores(jnp.minimum(k + 2, items - 1), k + 1)
            absorb(s_b, k + 1)
            return c

        lax.fori_loop(0, items // 2, pair, 0)

        @pl.when(items % 2 == 1)
        def _():
            absorb(s_a, items - 1)

    for qb in range(n_query):
        if last:
            total = l_all[qb]
            some = total > 0.0
            safe = jnp.where(some, total, 1.0)
            logsum = jnp.where(some, m_all[qb] + jnp.log2(safe), NEG)
            high = logsum.astype(jnp.bfloat16)
            rest = logsum - high.astype(jnp.float32)
            mid = rest.astype(jnp.bfloat16)
            low = (rest - mid.astype(jnp.float32)).astype(jnp.bfloat16)
            row = lax.broadcasted_iota(jnp.int32, (16, ROWS), 0)
            h2, m2, l2 = (jnp.concatenate([v, v], 0).astype(jnp.float32) for v in (high, mid, low))
            outs[qb][:D, :] = (acc_all[qb] / safe[:1]).astype(jnp.bfloat16)
            outs[qb][D:, :] = jnp.where(row == 0, h2, jnp.where(row == 1, m2, l2)).astype(jnp.bfloat16)
        else:
            outs[3 * qb][...], outs[3 * qb + 1][...] = m_all[qb], l_all[qb]

            def keep(i, carry, qb=qb):
                rows = pl.ds(pl.multiple_of(i * 16, 16), 16)
                outs[3 * qb + 2][rows, :] = acc_all[qb, rows, :]
                return carry

            lax.fori_loop(0, D // 16, keep, 0)


def run_chunk(work, steps, state, last, table, queries, messages):
    first = work[0] not in state
    sets = sorted({g for g, _ in work})
    n_query = len(work)
    n_keys = 256 * 2 * len(steps)
    keep = n_keys + TILE + 128
    max_items = n_query * (n_keys // TILE + 1) + 2
    shapes = [(8, ROWS), (8, ROWS), (D, ROWS)]
    smem = pl.BlockSpec(memory_space=pltpu.SMEM)
    vmem = pl.BlockSpec(memory_space=VMEM)
    operands = [table, *(queries[g] for g in sets), *messages]
    if not first:
        operands += [array for key in work for array in state[key]]
    if last:
        out_shape = [jax.ShapeDtypeStruct((OUT_ROWS, ROWS), jnp.bfloat16)] * n_query
    else:
        out_shape = [jax.ShapeDtypeStruct(s, jnp.float32) for s in shapes] * n_query
    pairs = n_query * n_keys * ROWS * 6 // 10
    name = "_".join(["attend", *(str(g) + "AB"[role] for g, role in work), str(len(steps))])
    results = pl.pallas_call(
        functools.partial(attend_chunk, tuple(work), tuple(sets), tuple(steps), first, last),
        out_shape=out_shape,
        in_specs=[smem] + [vmem] * (len(operands) - 1),
        out_specs=[vmem] * len(out_shape),
        scratch_shapes=[VMEM((n_query, *s), jnp.float32) for s in shapes]
        + [
            VMEM((n_query, ROWS, 2 * D), jnp.bfloat16),
            VMEM((keep, 2 * D), jnp.bfloat16),
            VMEM((keep, D), jnp.bfloat16),
            VMEM((TILE, ROWS), jnp.float32),
            VMEM((TILE, ROWS), jnp.float32),
            pltpu.SMEM((8,), jnp.int32),
            pltpu.SMEM((8,), jnp.int32),
            pltpu.SMEM((max_items,), jnp.int32),
            pltpu.SMEM((max_items,), jnp.int32),
        ],
        compiler_params=pltpu.CompilerParams(vmem_limit_bytes=24 * 2**20),
        cost_estimate=pl.CostEstimate(flops=pairs * 1024, bytes_accessed=8 * 2**20, transcendentals=pairs),
        name=name,
    )(*operands)
    if last:
        return results
    for i, key in enumerate(work):
        state[key] = tuple(results[3 * i : 3 * i + 3])
    return state


def project_body(table_ref, a_ref, b_ref, c_ref, d_ref, w_ref, give_ref, mine_ref, att):
    parts = (a_ref, b_ref, c_ref, d_ref)
    logs = []
    for part in parts:
        row = part[D:, :].astype(jnp.float32)
        logs.append(row[0:1] + row[1:2] + row[2:3])
    top = functools.reduce(jnp.maximum, logs)
    weights = [jnp.exp2(v - top) for v in logs]
    share = 1.0 / sum(weights)
    mixed = sum(part[:D, :].astype(jnp.float32) * (w * share) for part, w in zip(parts, weights))
    turned = mixed.T.astype(jnp.bfloat16)
    for h in range(HEADS):
        att[:, h * D : (h + 1) * D] = turned[h * BLK : (h + 1) * BLK, :]
    core = table_ref[PLACE + 4]
    half = BLK // 2
    wide = 512

    def columns(c, carry):
        cols = pl.ds(pl.multiple_of(c * wide, wide), wide)
        full = jnp.dot(att[...], w_ref[:, cols], preferred_element_type=jnp.float32)
        give_ref[:, cols] = jnp.where(core == 0, full[half:], full[:half]).astype(jnp.bfloat16)
        mine_ref[:, cols] = jnp.where(core == 0, full[:half], full[half:])
        return carry

    lax.fori_loop(0, w_ref.shape[1] // wide, columns, 0)


def project(table, parts, weight):
    vmem = pl.BlockSpec(memory_space=VMEM)
    wide = weight.shape[1]
    return pl.pallas_call(
        project_body,
        out_shape=(
            jax.ShapeDtypeStruct((BLK // 2, wide), jnp.bfloat16),
            jax.ShapeDtypeStruct((BLK // 2, wide), jnp.float32),
        ),
        in_specs=[pl.BlockSpec(memory_space=pltpu.SMEM)] + [vmem] * 5,
        out_specs=(vmem, vmem),
        scratch_shapes=[VMEM((BLK, HEADS * D), jnp.bfloat16)],
        compiler_params=pltpu.CompilerParams(vmem_limit_bytes=24 * 2**20),
        cost_estimate=pl.CostEstimate(flops=2 * BLK * HEADS * D * wide, bytes_accessed=12 * 2**20, transcendentals=0),
        name="project",
    )(table, *parts, weight)


def total_body(a_ref, b_ref, out):
    out[...] = (a_ref[...].astype(jnp.float32) + b_ref[...].astype(jnp.float32)).astype(out.dtype)


def total(a, b, dtype):
    vmem = pl.BlockSpec(memory_space=VMEM)
    return pl.pallas_call(
        total_body,
        out_shape=jax.ShapeDtypeStruct(a.shape, dtype),
        in_specs=[vmem] * 2,
        out_specs=vmem,
        compiler_params=pltpu.CompilerParams(vmem_limit_bytes=8 * 2**20),
        name="total",
    )(a, b)


def stage_body(src, dst):
    dst[...] = src[...]


def stage(array):
    vmem = pl.BlockSpec(memory_space=VMEM)
    return pl.pallas_call(
        stage_body,
        out_shape=jax.ShapeDtypeStruct(array.shape, array.dtype),
        in_specs=[vmem],
        out_specs=vmem,
        compiler_params=pltpu.CompilerParams(vmem_limit_bytes=8 * 2**20),
        name="stage",
    )(array)


def on_device(queries, window_keys, window_values, stored_keys, stored_values, block_order, window_offset, out_weight):
    x, yl, z = lax.axis_index("x"), lax.axis_index("yl"), lax.axis_index("z")
    core, yh = lax.axis_index("core"), lax.axis_index("yh")
    place = jnp.stack([x, yl, z, window_offset[0], core, yh]).astype(jnp.int32)
    table = jnp.concatenate([block_order, place])
    shard = jnp.concatenate([window_keys, stored_keys, window_values, stored_values], 0)

    def along(array, axis, size, to):
        return lax.ppermute(array, axis, [(i, to(i)) for i in range(size)])

    shard, queries = lax.optimization_barrier((shard, queries))
    other = along(shard, "x", 4, lambda i: 3 - i)
    base = jnp.concatenate([shard, other], 0)
    pair = [(a, b) for a in range(4) for b in range(2)]
    both = [(2 * a + b, 2 * (a ^ 1) + (1 - b)) for a, b in pair]
    to_member = [
        lambda v: v,
        lambda v: along(v, "x", 4, lambda i: i ^ 1),
        lambda v: along(v, "yl", 2, lambda i: 1 - i),
        lambda v: lax.ppermute(v, ("x", "yl"), both),
    ]
    q_sets = [queries] + [to_member[g](queries) for g in (1, 2, 3)]
    up = lambda a: along(a, "z", 8, lambda i: (i + 1) % 8)
    down = lambda a: along(a, "z", 8, lambda i: (i - 1) % 8)
    base, table, q_sets[0] = lax.optimization_barrier((base, table, stage(queries)))
    a1, b1 = up(base), down(base)
    a2, b2 = up(a1), down(b1)
    state = {}
    run = lambda work, steps, messages, last=False: run_chunk(work, steps, state, last, table, q_sets, messages)
    tie = lax.optimization_barrier
    near = (0, -1, 1), (base, a1, b1)
    A, B = 0, 1
    run([(0, A), (0, B)], *near)
    run([(3, A), (3, B)], *near)
    a2, b2, state[0, A], state[3, A] = tie((a2, b2, state[0, A], state[3, A]))
    a3, b3 = up(a2), down(b2)
    far = jnp.concatenate([up(a3[:SHARD]), down(b3[SHARD:])], 0)
    run([(1, A), (1, B), (2, A), (2, B)], *near)
    run([(g, r) for r in (A, B) for g in (1, 2, 3)], (-2, 2), (a2, b2))
    end = (-3, 3, 4), (a3, b3, far)
    sent_a = run([(3, A), (1, A), (2, A)], *end, True)
    *sent_a, state[3, B] = tie((*sent_a, state[3, B]))
    got_a = [to_member[g](v) for g, v in zip((3, 1, 2), sent_a)]
    sent_b = run([(3, B), (1, B), (2, B)], *end, True)
    got_b = [to_member[g](v) for g, v in zip((3, 1, 2), sent_b)]
    *got_a, state[0, A] = tie((*got_a, state[0, A]))
    rest = (-2, 2, -3, 3, 4), (a2, b2, a3, b3, far)
    (own_a,) = run([(0, A)], *rest, True)
    swap = lambda v, axis: along(v, axis, 2, lambda i: 1 - i)
    give_a, keep_a = project(table, (own_a, *got_a), out_weight)
    give_a, *got_b = tie((give_a, *got_b))
    sum_a = total(keep_a, swap(give_a, "core"), jnp.bfloat16)
    sum_a, state[0, B] = tie((sum_a, state[0, B]))
    across = swap(sum_a, "yh")
    (own_b,) = run([(0, B)], *rest, True)
    give_b, keep_b = project(table, (own_b, *got_b), out_weight)
    keep_b = total(keep_b, across, jnp.float32)
    return (keep_b + swap(give_b, "core").astype(jnp.float32)).astype(jnp.bfloat16)


def solution(mesh):
    fine = Mesh(mesh.devices.reshape(4, 2, 8, 2, 2), ("x", "yl", "z", "yh", "core"))
    ctx, tp = ("x", "yl", "z"), ("yh", "core")
    return jax.shard_map(
        on_device,
        mesh=fine,
        in_specs=(P(ctx, tp),) * 5 + (P(), P(), P(tp, None)),
        out_specs=P((*ctx, *tp), None),
        check_vma=False,
    )
```

```python
import functools

import jax
import jax.numpy as jnp
from jax import lax
from jax.experimental import pallas as pl
from jax.experimental.pallas import tpu as pltpu
from jax.sharding import Mesh, PartitionSpec as P

HEADS = 8
D = 128
BLK = 96
TOK = 2 * BLK
CACHE = 64
SHARD = 2 * (TOK + CACHE)
ROWS = HEADS * BLK
TILE = 384
NEG = -1e30
SCALE = D**-0.5 * 1.4426950408889634
PLACE = 128
OUT_ROWS = D + 16
NT = (((1,), (1,)), ((), ()))
TN = (((0,), (0,)), ((), ()))
VMEM = pltpu.VMEM


def attend_chunk(work, sets, steps, first, last, *refs):
    refs = list(refs)

    def take(count):
        taken = refs[:count]
        del refs[:count]
        return taken

    n_query = len(work)
    (table_ref,) = take(1)
    q_refs = take(len(sets))
    msgs = take(len(steps))
    old = [] if first else take(3 * n_query)
    outs = take(n_query if last else 3 * n_query)
    m_all, l_all, acc_all, qx, kx, vx, s_a, s_b, ends, marks, item_block, item_tile = refs
    x, yl, z, offset, yh = (table_ref[PLACE + i] for i in (0, 1, 2, 3, 5))
    n_keys = 256 * 2 * len(steps)

    token = lax.broadcasted_iota(jnp.int32, (BLK, D), 0)
    column = lax.broadcasted_iota(jnp.int32, (BLK, D), 1)
    hidden = ((column < BLK) & (column > token)) | (column == BLK)
    q_extra = jnp.where(hidden, NEG, 0.0).astype(jnp.bfloat16)
    own_rows = jnp.where(column == token, 1.0, 0.0).astype(jnp.bfloat16)
    half_of = [yh if role else 1 - yh for _, role in work]
    for qb, (g, role) in enumerate(work):
        src = q_refs[sets.index(g)]
        at = pl.ds(pl.multiple_of(half_of[qb] * BLK, 32), BLK)

        def stage_head(h, carry, qb=qb, src=src, at=at):
            rows = pl.ds(pl.multiple_of(h * BLK, 32), BLK)
            qx[qb, rows, :D] = src[at, pl.ds(pl.multiple_of(h * D, D), D)]
            qx[qb, rows, D:] = q_extra
            return carry

        lax.fori_loop(0, HEADS, stage_head, 0)

    def clear(i, carry):
        rows = pl.ds(pl.multiple_of(i * D, D), D)
        kx[rows, D:] = jnp.zeros((D, D), jnp.bfloat16)
        vx[rows, :] = jnp.zeros((D, D), jnp.bfloat16)
        return carry

    def clear_keys(i, carry):
        kx[pl.ds(pl.multiple_of(i * D, D), D), :D] = jnp.zeros((D, D), jnp.bfloat16)
        return carry

    lax.fori_loop(0, kx.shape[0] // D, clear, 0)
    lax.fori_loop(n_keys // D - len(steps), kx.shape[0] // D, clear_keys, 0)

    ctxs = []
    for step in steps:
        zz = lax.rem(z + step + 8, 8)
        ctxs += [x * 16 + yl * 8 + zz, (3 - x) * 16 + yl * 8 + zz]
    cache_rows = jnp.int32(0)
    slot = lax.broadcasted_iota(jnp.int32, (CACHE, D), 0)
    lane = lax.broadcasted_iota(jnp.int32, (CACHE, D), 1)
    for j, ctx in enumerate(ctxs):
        filled = offset - ctx * CACHE
        src = msgs[j // 2]
        base = (j % 2) * SHARD

        @pl.when(filled > 0)
        def _(src=src, base=base, at=cache_rows, filled=filled):
            to = pl.ds(pl.multiple_of(at, CACHE), CACHE)
            kx[to, :D] = src[base + TOK : base + TOK + CACHE, :]
            kx[to, D:] = jnp.where((slot >= filled) & (lane == BLK), 1.0, 0.0).astype(jnp.bfloat16)
            vx[to, :] = src[base + 2 * TOK + CACHE : base + SHARD, :]

        cache_rows = cache_rows + jnp.where(filled > 0, CACHE, 0)

    ids = [table_ref[2 * ctx + b] for ctx in ctxs for b in range(2)]
    ranks = [jnp.int32(0)] * len(ids)
    for j in range(len(ids)):
        for k in range(j):
            below = (ids[k] < ids[j]).astype(jnp.int32)
            ranks[j] = ranks[j] + below
            ranks[k] = ranks[k] + 1 - below
    for j, rank in enumerate(ranks):
        to = pl.ds(pl.multiple_of(cache_rows + rank * BLK, 32), BLK)
        src = msgs[j // 4]
        base = ((j // 2) % 2) * SHARD + (j % 2) * BLK
        kx[to, :D] = src[base : base + BLK, :]
        vx[to, :] = src[base + TOK + CACHE : base + TOK + CACHE + BLK, :]

    items = jnp.int32(0)
    for qb, (g, role) in enumerate(work):
        gx, gy = g % 2, g // 2
        q_x = x + 1 - 2 * lax.rem(x, 2) if gx else x
        q_y = 1 - yl if gy else yl
        q_id = table_ref[2 * (q_x * 16 + q_y * 8 + z) + half_of[qb]]
        count = jnp.int32(0)
        own = jnp.int32(0)
        for k in ids:
            count = count + (k <= q_id).astype(jnp.int32)
            own = own + (k == q_id).astype(jnp.int32)
        end = cache_rows + count * BLK
        ends[qb] = end
        marks[qb] = jnp.where(own > 0, end - BLK, n_keys + TILE)
        tiles = (end + TILE - 1) // TILE

        def add(t, at, qb=qb):
            item_block[at] = qb
            item_tile[at] = t
            return at + 1

        items = lax.fori_loop(0, tiles, add, items)
        if first:
            m_all[qb] = jnp.full((8, ROWS), NEG, jnp.float32)
            l_all[qb] = jnp.zeros((8, ROWS), jnp.float32)
            acc_all[qb] = jnp.zeros((D, ROWS), jnp.float32)
        else:
            m_all[qb], l_all[qb] = old[3 * qb][...], old[3 * qb + 1][...]

            def bring(i, carry, qb=qb):
                rows = pl.ds(pl.multiple_of(i * 16, 16), 16)
                acc_all[qb, rows, :] = old[3 * qb + 2][rows, :]
                return carry

            lax.fori_loop(0, D // 16, bring, 0)

    pad_lane = lax.broadcasted_iota(jnp.int32, (TILE, D), 1)
    pad_rows = jnp.where(pad_lane == BLK, 1.0, 0.0).astype(jnp.bfloat16)

    def scores(k, before):
        old, new = item_block[before], item_block[k]
        kx[pl.ds(pl.multiple_of(ends[old], 32), TILE), D:] = jnp.zeros_like(pad_rows)
        kx[pl.ds(pl.multiple_of(marks[old], 32), BLK), D:] = jnp.zeros_like(own_rows)
        kx[pl.ds(pl.multiple_of(ends[new], 32), TILE), D:] = pad_rows
        kx[pl.ds(pl.multiple_of(marks[new], 32), BLK), D:] = own_rows
        keys = kx[pl.ds(pl.multiple_of(item_tile[k] * TILE, TILE), TILE), :]
        return lax.dot_general(keys, qx[new], NT, preferred_element_type=jnp.float32)

    def absorb(s_ref, k):
        qb = item_block[k]
        s = s_ref[...]
        m0 = m_all[qb]
        m1 = jnp.maximum(m0, jnp.max(s, axis=0, keepdims=True) * SCALE)
        factor = jnp.exp2(m0 - m1)
        p = jnp.exp2(s * SCALE - m1[:1])
        l_all[qb] = l_all[qb] * factor + jnp.sum(p, axis=0, keepdims=True)
        m_all[qb] = m1
        values = vx[pl.ds(pl.multiple_of(item_tile[k] * TILE, TILE), TILE), :]
        acc_all[qb] = acc_all[qb] * factor[:1] + lax.dot_general(
            values, p.astype(jnp.bfloat16), TN, preferred_element_type=jnp.float32
        )

    @pl.when(items > 0)
    def _():
        s_a[...] = scores(0, 0)

        def pair(j, c):
            k = 2 * j
            s_b[...] = scores(k + 1, k)
            absorb(s_a, k)
            s_a[...] = scores(k + 2, k + 1)
            absorb(s_b, k + 1)
            return c

        lax.fori_loop(0, (items - 1) // 2, pair, 0)

        @pl.when(items % 2 == 0)
        def _():
            s_b[...] = scores(items - 1, items - 2)
            absorb(s_a, items - 2)

            def hand(i, c):
                rows = pl.ds(pl.multiple_of(i * 64, 64), 64)
                s_a[rows, :] = s_b[rows, :]
                return c

            lax.fori_loop(0, TILE // 64, hand, 0)

        absorb(s_a, items - 1)

    for qb in range(n_query):
        if last:
            total = l_all[qb]
            some = total > 0.0
            safe = jnp.where(some, total, 1.0)
            logsum = jnp.where(some, m_all[qb] + jnp.log2(safe), NEG)
            high = logsum.astype(jnp.bfloat16)
            rest = logsum - high.astype(jnp.float32)
            mid = rest.astype(jnp.bfloat16)
            low = (rest - mid.astype(jnp.float32)).astype(jnp.bfloat16)
            row = lax.broadcasted_iota(jnp.int32, (16, ROWS), 0)
            h2, m2, l2 = (jnp.concatenate([v, v], 0).astype(jnp.float32) for v in (high, mid, low))
            outs[qb][:D, :] = (acc_all[qb] / safe[:1]).astype(jnp.bfloat16)
            outs[qb][D:, :] = jnp.where(row == 0, h2, jnp.where(row == 1, m2, l2)).astype(jnp.bfloat16)
        else:
            outs[3 * qb][...], outs[3 * qb + 1][...] = m_all[qb], l_all[qb]

            def keep(i, carry, qb=qb):
                rows = pl.ds(pl.multiple_of(i * 16, 16), 16)
                outs[3 * qb + 2][rows, :] = acc_all[qb, rows, :]
                return carry

            lax.fori_loop(0, D // 16, keep, 0)


def run_chunk(work, steps, state, last, table, queries, messages):
    first = work[0] not in state
    sets = sorted({g for g, _ in work})
    n_query = len(work)
    n_keys = 256 * 2 * len(steps)
    keep = n_keys + TILE + 128
    max_items = n_query * (n_keys // TILE + 1) + 2
    shapes = [(8, ROWS), (8, ROWS), (D, ROWS)]
    smem = pl.BlockSpec(memory_space=pltpu.SMEM)
    vmem = pl.BlockSpec(memory_space=VMEM)
    operands = [table, *(queries[g] for g in sets), *messages]
    if not first:
        operands += [array for key in work for array in state[key]]
    if last:
        out_shape = [jax.ShapeDtypeStruct((OUT_ROWS, ROWS), jnp.bfloat16)] * n_query
    else:
        out_shape = [jax.ShapeDtypeStruct(s, jnp.float32) for s in shapes] * n_query
    pairs = n_query * n_keys * ROWS * 6 // 10
    name = "_".join(["attend", *(str(g) + "AB"[role] for g, role in work), str(len(steps))])
    results = pl.pallas_call(
        functools.partial(attend_chunk, tuple(work), tuple(sets), tuple(steps), first, last),
        out_shape=out_shape,
        in_specs=[smem] + [vmem] * (len(operands) - 1),
        out_specs=[vmem] * len(out_shape),
        scratch_shapes=[VMEM((n_query, *s), jnp.float32) for s in shapes]
        + [
            VMEM((n_query, ROWS, 2 * D), jnp.bfloat16),
            VMEM((keep, 2 * D), jnp.bfloat16),
            VMEM((keep, D), jnp.bfloat16),
            VMEM((TILE, ROWS), jnp.float32),
            VMEM((TILE, ROWS), jnp.float32),
            pltpu.SMEM((8,), jnp.int32),
            pltpu.SMEM((8,), jnp.int32),
            pltpu.SMEM((max_items,), jnp.int32),
            pltpu.SMEM((max_items,), jnp.int32),
        ],
        compiler_params=pltpu.CompilerParams(vmem_limit_bytes=24 * 2**20),
        cost_estimate=pl.CostEstimate(flops=pairs * 1024, bytes_accessed=8 * 2**20, transcendentals=pairs),
        name=name,
    )(*operands)
    if last:
        return results
    for i, key in enumerate(work):
        state[key] = tuple(results[3 * i : 3 * i + 3])
    return state


def project_body(table_ref, a_ref, b_ref, c_ref, d_ref, w_ref, give_ref, mine_ref, att):
    parts = (a_ref, b_ref, c_ref, d_ref)
    logs = []
    for part in parts:
        row = part[D:, :].astype(jnp.float32)
        logs.append(row[0:1] + row[1:2] + row[2:3])
    top = functools.reduce(jnp.maximum, logs)
    weights = [jnp.exp2(v - top) for v in logs]
    share = 1.0 / sum(weights)
    mixed = sum(part[:D, :].astype(jnp.float32) * (w * share) for part, w in zip(parts, weights))
    turned = mixed.T.astype(jnp.bfloat16)
    for h in range(HEADS):
        att[:, h * D : (h + 1) * D] = turned[h * BLK : (h + 1) * BLK, :]
    core = table_ref[PLACE + 4]
    half = BLK // 2
    wide = 512

    def columns(c, carry):
        cols = pl.ds(pl.multiple_of(c * wide, wide), wide)
        full = jnp.dot(att[...], w_ref[:, cols], preferred_element_type=jnp.float32)
        give_ref[:, cols] = jnp.where(core == 0, full[half:], full[:half]).astype(jnp.bfloat16)
        mine_ref[:, cols] = jnp.where(core == 0, full[:half], full[half:])
        return carry

    lax.fori_loop(0, w_ref.shape[1] // wide, columns, 0)


def project(table, parts, weight):
    vmem = pl.BlockSpec(memory_space=VMEM)
    wide = weight.shape[1]
    return pl.pallas_call(
        project_body,
        out_shape=(
            jax.ShapeDtypeStruct((BLK // 2, wide), jnp.bfloat16),
            jax.ShapeDtypeStruct((BLK // 2, wide), jnp.float32),
        ),
        in_specs=[pl.BlockSpec(memory_space=pltpu.SMEM)] + [vmem] * 5,
        out_specs=(vmem, vmem),
        scratch_shapes=[VMEM((BLK, HEADS * D), jnp.bfloat16)],
        compiler_params=pltpu.CompilerParams(vmem_limit_bytes=24 * 2**20),
        cost_estimate=pl.CostEstimate(flops=2 * BLK * HEADS * D * wide, bytes_accessed=12 * 2**20, transcendentals=0),
        name="project",
    )(table, *parts, weight)


def total_body(a_ref, b_ref, out):
    out[...] = (a_ref[...].astype(jnp.float32) + b_ref[...].astype(jnp.float32)).astype(out.dtype)


def total(a, b, dtype):
    vmem = pl.BlockSpec(memory_space=VMEM)
    return pl.pallas_call(
        total_body,
        out_shape=jax.ShapeDtypeStruct(a.shape, dtype),
        in_specs=[vmem] * 2,
        out_specs=vmem,
        compiler_params=pltpu.CompilerParams(vmem_limit_bytes=8 * 2**20),
        name="total",
    )(a, b)


def stage_body(src, dst):
    dst[...] = src[...]


def stage(array):
    vmem = pl.BlockSpec(memory_space=VMEM)
    return pl.pallas_call(
        stage_body,
        out_shape=jax.ShapeDtypeStruct(array.shape, array.dtype),
        in_specs=[vmem],
        out_specs=vmem,
        compiler_params=pltpu.CompilerParams(vmem_limit_bytes=8 * 2**20),
        name="stage",
    )(array)


def on_device(queries, window_keys, window_values, stored_keys, stored_values, block_order, window_offset, out_weight):
    x, yl, z = lax.axis_index("x"), lax.axis_index("yl"), lax.axis_index("z")
    core, yh = lax.axis_index("core"), lax.axis_index("yh")
    place = jnp.stack([x, yl, z, window_offset[0], core, yh]).astype(jnp.int32)
    table = jnp.concatenate([block_order, place])
    shard = jnp.concatenate([window_keys, stored_keys, window_values, stored_values], 0)

    def along(array, axis, size, to):
        return lax.ppermute(array, axis, [(i, to(i)) for i in range(size)])

    shard, queries = lax.optimization_barrier((shard, queries))
    other = along(shard, "x", 4, lambda i: 3 - i)
    base = jnp.concatenate([shard, other], 0)
    pair = [(a, b) for a in range(4) for b in range(2)]
    both = [(2 * a + b, 2 * (a ^ 1) + (1 - b)) for a, b in pair]
    to_member = [
        lambda v: v,
        lambda v: along(v, "x", 4, lambda i: i ^ 1),
        lambda v: along(v, "yl", 2, lambda i: 1 - i),
        lambda v: lax.ppermute(v, ("x", "yl"), both),
    ]
    q_sets = [queries] + [to_member[g](queries) for g in (1, 2, 3)]
    up = lambda a: along(a, "z", 8, lambda i: (i + 1) % 8)
    down = lambda a: along(a, "z", 8, lambda i: (i - 1) % 8)
    base, table, q_sets[0] = lax.optimization_barrier((base, table, stage(queries)))
    a1, b1 = up(base), down(base)
    a2, b2 = up(a1), down(b1)
    state = {}
    run = lambda work, steps, messages, last=False: run_chunk(work, steps, state, last, table, q_sets, messages)
    tie = lax.optimization_barrier
    near = (0, -1, 1), (base, a1, b1)
    A, B = 0, 1
    run([(0, A), (0, B)], *near)
    run([(3, A), (3, B)], *near)
    a2, b2, state[0, A], state[3, A] = tie((a2, b2, state[0, A], state[3, A]))
    a3, b3 = up(a2), down(b2)
    far = jnp.concatenate([up(a3[:SHARD]), down(b3[SHARD:])], 0)
    run([(1, A), (1, B), (2, A), (2, B)], *near)
    run([(g, r) for r in (A, B) for g in (1, 2, 3)], (-2, 2), (a2, b2))
    end = (-3, 3, 4), (a3, b3, far)
    sent_a = run([(3, A), (1, A), (2, A)], *end, True)
    *sent_a, state[3, B] = tie((*sent_a, state[3, B]))
    got_a = [to_member[g](v) for g, v in zip((3, 1, 2), sent_a)]
    sent_b = run([(3, B), (1, B), (2, B)], *end, True)
    got_b = [to_member[g](v) for g, v in zip((3, 1, 2), sent_b)]
    *got_a, state[0, A] = tie((*got_a, state[0, A]))
    rest = (-2, 2, -3, 3, 4), (a2, b2, a3, b3, far)
    (own_a,) = run([(0, A)], *rest, True)
    swap = lambda v, axis: along(v, axis, 2, lambda i: 1 - i)
    give_a, keep_a = project(table, (own_a, *got_a), out_weight)
    give_a, *got_b = tie((give_a, *got_b))
    sum_a = total(keep_a, swap(give_a, "core"), jnp.bfloat16)
    sum_a, state[0, B] = tie((sum_a, state[0, B]))
    across = swap(sum_a, "yh")
    (own_b,) = run([(0, B)], *rest, True)
    give_b, keep_b = project(table, (own_b, *got_b), out_weight)
    keep_b = total(keep_b, across, jnp.float32)
    return (keep_b + swap(give_b, "core").astype(jnp.float32)).astype(jnp.bfloat16)


def solution(mesh):
    fine = Mesh(mesh.devices.reshape(4, 2, 8, 2, 2), ("x", "yl", "z", "yh", "core"))
    ctx, tp = ("x", "yl", "z"), ("yh", "core")
    return jax.shard_map(
        on_device,
        mesh=fine,
        in_specs=(P(ctx, tp),) * 5 + (P(), P(), P(tp, None)),
        out_specs=P((*ctx, *tp), None),
        check_vma=False,
    )
```

```python
import functools

import jax
import jax.numpy as jnp
from jax import lax
from jax.experimental import pallas as pl
from jax.experimental.pallas import tpu as pltpu
from jax.sharding import Mesh, PartitionSpec as P

HEADS = 8
D = 128
BLK = 96
TOK = 2 * BLK
CACHE = 64
SHARD = 2 * (TOK + CACHE)
ROWS = HEADS * BLK
TILE = 384
NEG = -1e30
SCALE = D**-0.5 * 1.4426950408889634
PLACE = 128
OUT_ROWS = D + 16
NT = (((1,), (1,)), ((), ()))
TN = (((0,), (0,)), ((), ()))
VMEM = pltpu.VMEM


def attend_chunk(work, sets, steps, first, last, *refs):
    refs = list(refs)

    def take(count):
        taken = refs[:count]
        del refs[:count]
        return taken

    n_query = len(work)
    (table_ref,) = take(1)
    q_refs = take(len(sets))
    msgs = take(len(steps))
    old = [] if first else take(3 * n_query)
    outs = take(n_query if last else 3 * n_query)
    m_all, l_all, acc_all, qx, kx, vx, s_a, s_b, ends, marks, item_block, item_tile = refs
    x, yl, z, offset, yh = (table_ref[PLACE + i] for i in (0, 1, 2, 3, 5))
    n_keys = 256 * 2 * len(steps)

    token = lax.broadcasted_iota(jnp.int32, (BLK, D), 0)
    column = lax.broadcasted_iota(jnp.int32, (BLK, D), 1)
    hidden = ((column < BLK) & (column > token)) | (column == BLK)
    q_extra = jnp.where(hidden, NEG, 0.0).astype(jnp.bfloat16)
    own_rows = jnp.where(column == token, 1.0, 0.0).astype(jnp.bfloat16)
    half_of = [yh if role else 1 - yh for _, role in work]
    for qb, (g, role) in enumerate(work):
        src = q_refs[sets.index(g)]
        at = pl.ds(pl.multiple_of(half_of[qb] * BLK, 32), BLK)

        def stage_head(h, carry, qb=qb, src=src, at=at):
            rows = pl.ds(pl.multiple_of(h * BLK, 32), BLK)
            qx[qb, rows, :D] = src[at, pl.ds(pl.multiple_of(h * D, D), D)]
            qx[qb, rows, D:] = q_extra
            return carry

        lax.fori_loop(0, HEADS, stage_head, 0, unroll=4)

    def clear(i, carry):
        rows = pl.ds(pl.multiple_of(i * D, D), D)
        kx[rows, D:] = jnp.zeros((D, D), jnp.bfloat16)
        vx[rows, :] = jnp.zeros((D, D), jnp.bfloat16)
        return carry

    def clear_keys(i, carry):
        kx[pl.ds(pl.multiple_of(i * D, D), D), :D] = jnp.zeros((D, D), jnp.bfloat16)
        return carry

    lax.fori_loop(0, kx.shape[0] // D, clear, 0)
    lax.fori_loop(n_keys // D - len(steps), kx.shape[0] // D, clear_keys, 0)

    ctxs = []
    for step in steps:
        zz = lax.rem(z + step + 8, 8)
        ctxs += [x * 16 + yl * 8 + zz, (3 - x) * 16 + yl * 8 + zz]
    cache_rows = jnp.int32(0)
    slot = lax.broadcasted_iota(jnp.int32, (CACHE, D), 0)
    lane = lax.broadcasted_iota(jnp.int32, (CACHE, D), 1)
    for j, ctx in enumerate(ctxs):
        filled = offset - ctx * CACHE
        src = msgs[j // 2]
        base = (j % 2) * SHARD

        @pl.when(filled > 0)
        def _(src=src, base=base, at=cache_rows, filled=filled):
            to = pl.ds(pl.multiple_of(at, CACHE), CACHE)
            kx[to, :D] = src[base + TOK : base + TOK + CACHE, :]
            kx[to, D:] = jnp.where((slot >= filled) & (lane == BLK), 1.0, 0.0).astype(jnp.bfloat16)
            vx[to, :] = src[base + 2 * TOK + CACHE : base + SHARD, :]

        cache_rows = cache_rows + jnp.where(filled > 0, CACHE, 0)

    ids = [table_ref[2 * ctx + b] for ctx in ctxs for b in range(2)]
    ranks = [jnp.int32(0)] * len(ids)
    for j in range(len(ids)):
        for k in range(j):
            below = (ids[k] < ids[j]).astype(jnp.int32)
            ranks[j] = ranks[j] + below
            ranks[k] = ranks[k] + 1 - below
    for j, rank in enumerate(ranks):
        to = pl.ds(pl.multiple_of(cache_rows + rank * BLK, 32), BLK)
        src = msgs[j // 4]
        base = ((j // 2) % 2) * SHARD + (j % 2) * BLK
        kx[to, :D] = src[base : base + BLK, :]
        vx[to, :] = src[base + TOK + CACHE : base + TOK + CACHE + BLK, :]

    items = jnp.int32(0)
    for qb, (g, role) in enumerate(work):
        gx, gy = g % 2, g // 2
        q_x = x + 1 - 2 * lax.rem(x, 2) if gx else x
        q_y = 1 - yl if gy else yl
        q_id = table_ref[2 * (q_x * 16 + q_y * 8 + z) + half_of[qb]]
        count = jnp.int32(0)
        own = jnp.int32(0)
        for k in ids:
            count = count + (k <= q_id).astype(jnp.int32)
            own = own + (k == q_id).astype(jnp.int32)
        end = cache_rows + count * BLK
        ends[qb] = end
        marks[qb] = jnp.where(own > 0, end - BLK, n_keys + TILE)
        tiles = (end + TILE - 1) // TILE

        def add(t, at, qb=qb):
            item_block[at] = qb
            item_tile[at] = t
            return at + 1

        items = lax.fori_loop(0, tiles, add, items)
        if first:
            m_all[qb] = jnp.full((8, ROWS), NEG, jnp.float32)
            l_all[qb] = jnp.zeros((8, ROWS), jnp.float32)
            acc_all[qb] = jnp.zeros((D, ROWS), jnp.float32)
        else:
            m_all[qb], l_all[qb] = old[3 * qb][...], old[3 * qb + 1][...]

            def bring(i, carry, qb=qb):
                rows = pl.ds(pl.multiple_of(i * 64, 64), 64)
                acc_all[qb, rows, :] = old[3 * qb + 2][rows, :]
                return carry

            lax.fori_loop(0, D // 64, bring, 0)

    pad_lane = lax.broadcasted_iota(jnp.int32, (TILE, D), 1)
    pad_rows = jnp.where(pad_lane == BLK, 1.0, 0.0).astype(jnp.bfloat16)

    def scores(k, before):
        old, new = item_block[before], item_block[k]
        kx[pl.ds(pl.multiple_of(ends[old], 32), TILE), D:] = jnp.zeros_like(pad_rows)
        kx[pl.ds(pl.multiple_of(marks[old], 32), BLK), D:] = jnp.zeros_like(own_rows)
        kx[pl.ds(pl.multiple_of(ends[new], 32), TILE), D:] = pad_rows
        kx[pl.ds(pl.multiple_of(marks[new], 32), BLK), D:] = own_rows
        keys = kx[pl.ds(pl.multiple_of(item_tile[k] * TILE, TILE), TILE), :]
        return lax.dot_general(keys, qx[new], NT, preferred_element_type=jnp.float32)

    def absorb(s_ref, k):
        qb = item_block[k]
        s = s_ref[...]
        m0 = m_all[qb]
        m1 = jnp.maximum(m0, jnp.max(s, axis=0, keepdims=True) * SCALE)
        factor = jnp.exp2(m0 - m1)
        p = jnp.exp2(s * SCALE - m1[:1])
        l_all[qb] = l_all[qb] * factor + jnp.sum(p, axis=0, keepdims=True)
        m_all[qb] = m1
        values = vx[pl.ds(pl.multiple_of(item_tile[k] * TILE, TILE), TILE), :]
        acc_all[qb] = acc_all[qb] * factor[:1] + lax.dot_general(
            values, p.astype(jnp.bfloat16), TN, preferred_element_type=jnp.float32
        )

    @pl.when(items > 0)
    def _():
        s_a[...] = scores(0, 0)

        def pair(j, c):
            k = 2 * j
            s_b[...] = scores(k + 1, k)
            absorb(s_a, k)
            s_a[...] = scores(k + 2, k + 1)
            absorb(s_b, k + 1)
            return c

        lax.fori_loop(0, (items - 1) // 2, pair, 0)

        @pl.when(items % 2 == 0)
        def _():
            s_b[...] = scores(items - 1, items - 2)
            absorb(s_a, items - 2)

            def hand(i, c):
                rows = pl.ds(pl.multiple_of(i * 64, 64), 64)
                s_a[rows, :] = s_b[rows, :]
                return c

            lax.fori_loop(0, TILE // 64, hand, 0)

        absorb(s_a, items - 1)

    for qb in range(n_query):
        if last:
            total = l_all[qb]
            some = total > 0.0
            safe = jnp.where(some, total, 1.0)
            logsum = jnp.where(some, m_all[qb] + jnp.log2(safe), NEG)
            high = logsum.astype(jnp.bfloat16)
            rest = logsum - high.astype(jnp.float32)
            mid = rest.astype(jnp.bfloat16)
            low = (rest - mid.astype(jnp.float32)).astype(jnp.bfloat16)
            row = lax.broadcasted_iota(jnp.int32, (16, ROWS), 0)
            h2, m2, l2 = (jnp.concatenate([v, v], 0).astype(jnp.float32) for v in (high, mid, low))
            outs[qb][:D, :] = (acc_all[qb] / safe[:1]).astype(jnp.bfloat16)
            outs[qb][D:, :] = jnp.where(row == 0, h2, jnp.where(row == 1, m2, l2)).astype(jnp.bfloat16)
        else:
            outs[3 * qb][...], outs[3 * qb + 1][...] = m_all[qb], l_all[qb]

            def keep(i, carry, qb=qb):
                rows = pl.ds(pl.multiple_of(i * 64, 64), 64)
                outs[3 * qb + 2][rows, :] = acc_all[qb, rows, :]
                return carry

            lax.fori_loop(0, D // 64, keep, 0)


def run_chunk(work, steps, state, last, table, queries, messages):
    first = work[0] not in state
    sets = sorted({g for g, _ in work})
    n_query = len(work)
    n_keys = 256 * 2 * len(steps)
    keep = n_keys + TILE + 128
    max_items = n_query * (n_keys // TILE + 1) + 2
    shapes = [(8, ROWS), (8, ROWS), (D, ROWS)]
    smem = pl.BlockSpec(memory_space=pltpu.SMEM)
    vmem = pl.BlockSpec(memory_space=VMEM)
    operands = [table, *(queries[g] for g in sets), *messages]
    if not first:
        operands += [array for key in work for array in state[key]]
    if last:
        out_shape = [jax.ShapeDtypeStruct((OUT_ROWS, ROWS), jnp.bfloat16)] * n_query
    else:
        out_shape = [jax.ShapeDtypeStruct(s, jnp.float32) for s in shapes] * n_query
    pairs = n_query * n_keys * ROWS * 6 // 10
    name = "_".join(["attend", *(str(g) + "AB"[role] for g, role in work), str(len(steps))])
    results = pl.pallas_call(
        functools.partial(attend_chunk, tuple(work), tuple(sets), tuple(steps), first, last),
        out_shape=out_shape,
        in_specs=[smem] + [vmem] * (len(operands) - 1),
        out_specs=[vmem] * len(out_shape),
        scratch_shapes=[VMEM((n_query, *s), jnp.float32) for s in shapes]
        + [
            VMEM((n_query, ROWS, 2 * D), jnp.bfloat16),
            VMEM((keep, 2 * D), jnp.bfloat16),
            VMEM((keep, D), jnp.bfloat16),
            VMEM((TILE, ROWS), jnp.float32),
            VMEM((TILE, ROWS), jnp.float32),
            pltpu.SMEM((8,), jnp.int32),
            pltpu.SMEM((8,), jnp.int32),
            pltpu.SMEM((max_items,), jnp.int32),
            pltpu.SMEM((max_items,), jnp.int32),
        ],
        compiler_params=pltpu.CompilerParams(vmem_limit_bytes=24 * 2**20),
        cost_estimate=pl.CostEstimate(
            flops=1024 if sets == [0] else pairs * 1024, bytes_accessed=1024 if sets == [0] else 8 * 2**20, transcendentals=0
        ),
        name=name,
    )(*operands)
    if last:
        return results
    for i, key in enumerate(work):
        state[key] = tuple(results[3 * i : 3 * i + 3])
    return state


def project_body(table_ref, a_ref, b_ref, c_ref, d_ref, w_ref, give_ref, mine_ref, att):
    parts = (a_ref, b_ref, c_ref, d_ref)
    logs = []
    for part in parts:
        row = part[D:, :].astype(jnp.float32)
        logs.append(row[0:1] + row[1:2] + row[2:3])
    top = functools.reduce(jnp.maximum, logs)
    weights = [jnp.exp2(v - top) for v in logs]
    share = 1.0 / sum(weights)
    mixed = sum(part[:D, :].astype(jnp.float32) * (w * share) for part, w in zip(parts, weights))
    turned = mixed.T.astype(jnp.bfloat16)
    for h in range(HEADS):
        att[:, h * D : (h + 1) * D] = turned[h * BLK : (h + 1) * BLK, :]
    core = table_ref[PLACE + 4]
    half = BLK // 2
    wide = 1024

    def columns(c, carry):
        cols = pl.ds(pl.multiple_of(c * wide, wide), wide)
        full = jnp.dot(att[...], w_ref[:, cols], preferred_element_type=jnp.float32)
        give_ref[:, cols] = jnp.where(core == 0, full[half:], full[:half]).astype(jnp.bfloat16)
        mine_ref[:, cols] = jnp.where(core == 0, full[:half], full[half:])
        return carry

    lax.fori_loop(0, w_ref.shape[1] // wide, columns, 0)


def project(table, parts, weight):
    vmem = pl.BlockSpec(memory_space=VMEM)
    wide = weight.shape[1]
    return pl.pallas_call(
        project_body,
        out_shape=(
            jax.ShapeDtypeStruct((BLK // 2, wide), jnp.bfloat16),
            jax.ShapeDtypeStruct((BLK // 2, wide), jnp.float32),
        ),
        in_specs=[pl.BlockSpec(memory_space=pltpu.SMEM)] + [vmem] * 5,
        out_specs=(vmem, vmem),
        scratch_shapes=[VMEM((BLK, HEADS * D), jnp.bfloat16)],
        compiler_params=pltpu.CompilerParams(vmem_limit_bytes=24 * 2**20),
        cost_estimate=pl.CostEstimate(flops=2 * BLK * HEADS * D * wide, bytes_accessed=12 * 2**20, transcendentals=0),
        name="project",
    )(table, *parts, weight)


def total_body(a_ref, b_ref, out):
    out[...] = (a_ref[...].astype(jnp.float32) + b_ref[...].astype(jnp.float32)).astype(out.dtype)


def total(a, b, dtype):
    vmem = pl.BlockSpec(memory_space=VMEM)
    return pl.pallas_call(
        total_body,
        out_shape=jax.ShapeDtypeStruct(a.shape, dtype),
        in_specs=[vmem] * 2,
        out_specs=vmem,
        compiler_params=pltpu.CompilerParams(vmem_limit_bytes=8 * 2**20),
        name="total",
    )(a, b)


def stage_body(src, dst):
    dst[...] = src[...]


def stage(array):
    vmem = pl.BlockSpec(memory_space=VMEM)
    return pl.pallas_call(
        stage_body,
        out_shape=jax.ShapeDtypeStruct(array.shape, array.dtype),
        in_specs=[vmem],
        out_specs=vmem,
        compiler_params=pltpu.CompilerParams(vmem_limit_bytes=8 * 2**20),
        name="stage",
    )(array)


def on_device(queries, window_keys, window_values, stored_keys, stored_values, block_order, window_offset, out_weight):
    x, yl, z = lax.axis_index("x"), lax.axis_index("yl"), lax.axis_index("z")
    core, yh = lax.axis_index("core"), lax.axis_index("yh")
    place = jnp.stack([x, yl, z, window_offset[0], core, yh]).astype(jnp.int32)
    table = jnp.concatenate([block_order, place])
    shard = jnp.concatenate([window_keys, stored_keys, window_values, stored_values], 0)

    def along(array, axis, size, to):
        return lax.ppermute(array, axis, [(i, to(i)) for i in range(size)])

    shard, queries = lax.optimization_barrier((shard, queries))
    other = along(shard, "x", 4, lambda i: 3 - i)
    base = jnp.concatenate([shard, other], 0)
    pair = [(a, b) for a in range(4) for b in range(2)]
    both = [(2 * a + b, 2 * (a ^ 1) + (1 - b)) for a, b in pair]
    to_member = [
        lambda v: v,
        lambda v: along(v, "x", 4, lambda i: i ^ 1),
        lambda v: along(v, "yl", 2, lambda i: 1 - i),
        lambda v: lax.ppermute(v, ("x", "yl"), both),
    ]
    q_sets = [queries] + [to_member[g](queries) for g in (1, 2, 3)]
    up = lambda a: along(a, "z", 8, lambda i: (i + 1) % 8)
    down = lambda a: along(a, "z", 8, lambda i: (i - 1) % 8)
    base, table, q_sets[0] = lax.optimization_barrier((base, table, stage(queries)))
    a1, b1 = up(base), down(base)
    a2, b2 = up(a1), down(b1)
    state = {}
    run = lambda work, steps, messages, last=False: run_chunk(work, steps, state, last, table, q_sets, messages)
    tie = lax.optimization_barrier
    near = (0, -1, 1), (base, a1, b1)
    A, B = 0, 1
    run([(0, A), (0, B)], *near)
    run([(3, A), (3, B)], *near)
    a2, b2, state[0, A], state[3, A] = tie((a2, b2, state[0, A], state[3, A]))
    a3, b3 = up(a2), down(b2)
    far = jnp.concatenate([up(a3[:SHARD]), down(b3[SHARD:])], 0)
    run([(1, A), (1, B), (2, A), (2, B)], *near)
    run([(g, r) for r in (A, B) for g in (1, 2, 3)], (-2, 2), (a2, b2))
    end = (-3, 3, 4), (a3, b3, far)
    sent_a = run([(3, A), (1, A), (2, A)], *end, True)
    *sent_a, state[3, B] = tie((*sent_a, state[3, B]))
    got_a = [to_member[g](v) for g, v in zip((3, 1, 2), sent_a)]
    sent_b = run([(3, B), (1, B), (2, B)], *end, True)
    *sent_b, state[0, A] = tie((*sent_b, state[0, A]))
    got_b = [to_member[g](v) for g, v in zip((3, 1, 2), sent_b)]
    rest = (-2, 2, -3, 3, 4), (a2, b2, a3, b3, far)
    (own_a,) = run([(0, A)], *rest, True)
    swap = lambda v, axis: along(v, axis, 2, lambda i: 1 - i)
    give_a, keep_a = project(table, (own_a, *got_a), out_weight)
    give_a, *got_b = tie((give_a, *got_b))
    sum_a = total(keep_a, swap(give_a, "core"), jnp.bfloat16)
    sum_a, state[0, B] = tie((sum_a, state[0, B]))
    across = swap(sum_a, "yh")
    (own_b,) = run([(0, B)], *rest, True)
    give_b, keep_b = project(table, (own_b, *got_b), out_weight)
    keep_b = total(keep_b, across, jnp.float32)
    return (keep_b + swap(give_b, "core").astype(jnp.float32)).astype(jnp.bfloat16)


def solution(mesh):
    fine = Mesh(mesh.devices.reshape(4, 2, 8, 2, 2), ("x", "yl", "z", "yh", "core"))
    ctx, tp = ("x", "yl", "z"), ("yh", "core")
    return jax.shard_map(
        on_device,
        mesh=fine,
        in_specs=(P(ctx, tp),) * 5 + (P(), P(), P(tp, None)),
        out_specs=P((*ctx, *tp), None),
        check_vma=False,
    )
```

```python
import functools

import jax
import jax.numpy as jnp
from jax import lax
from jax.experimental import pallas as pl
from jax.experimental.pallas import tpu as pltpu
from jax.sharding import Mesh, PartitionSpec as P

HEADS = 8
D = 128
BLK = 96
TOK = 2 * BLK
CACHE = 64
SHARD = 2 * (TOK + CACHE)
ROWS = HEADS * BLK
TILE = 384
NEG = -1e30
SCALE = D**-0.5 * 1.4426950408889634
PLACE = 128
OUT_ROWS = D + 16
NT = (((1,), (1,)), ((), ()))
TN = (((0,), (0,)), ((), ()))
VMEM = pltpu.VMEM


def attend_chunk(work, sets, steps, first, last, *refs):
    refs = list(refs)

    def take(count):
        taken = refs[:count]
        del refs[:count]
        return taken

    n_query = len(work)
    (table_ref,) = take(1)
    q_refs = take(len(sets))
    msgs = take(len(steps))
    old = [] if first else take(3 * n_query)
    outs = take(n_query if last else 3 * n_query)
    m_all, l_all, acc_all, qx, kx, vx, s_a, s_b, top_a, top_b, ends, marks, item_block, item_tile = refs
    x, yl, z, offset, yh = (table_ref[PLACE + i] for i in (0, 1, 2, 3, 5))
    n_keys = 256 * 2 * len(steps)

    token = lax.broadcasted_iota(jnp.int32, (BLK, D), 0)
    column = lax.broadcasted_iota(jnp.int32, (BLK, D), 1)
    hidden = ((column < BLK) & (column > token)) | (column == BLK)
    q_extra = jnp.where(hidden, NEG, 0.0).astype(jnp.bfloat16)
    own_rows = jnp.where(column == token, 1.0, 0.0).astype(jnp.bfloat16)
    half_of = [yh if role else 1 - yh for _, role in work]
    for qb, (g, role) in enumerate(work):
        src = q_refs[sets.index(g)]
        at = pl.ds(pl.multiple_of(half_of[qb] * BLK, 32), BLK)

        def stage_head(h, carry, qb=qb, src=src, at=at):
            rows = pl.ds(pl.multiple_of(h * BLK, 32), BLK)
            qx[qb, rows, :D] = src[at, pl.ds(pl.multiple_of(h * D, D), D)]
            qx[qb, rows, D:] = q_extra
            return carry

        lax.fori_loop(0, HEADS, stage_head, 0, unroll=4)

    def clear_marks(i, carry):
        rows = pl.ds(pl.multiple_of(i * D, D), D)
        kx[rows, D:] = jnp.zeros((D, D), jnp.bfloat16)
        return carry

    def clear_tail(i, carry):
        rows = pl.ds(pl.multiple_of(i * D, D), D)
        kx[rows, :D] = jnp.zeros((D, D), jnp.bfloat16)
        vx[rows, :] = jnp.zeros((D, D), jnp.bfloat16)
        return carry

    lax.fori_loop(0, kx.shape[0] // D, clear_marks, 0)
    lax.fori_loop(n_keys // D - len(steps), kx.shape[0] // D, clear_tail, 0)

    ctxs = []
    for step in steps:
        zz = lax.rem(z + step + 8, 8)
        ctxs += [x * 16 + yl * 8 + zz, (3 - x) * 16 + yl * 8 + zz]
    cache_rows = jnp.int32(0)
    slot = lax.broadcasted_iota(jnp.int32, (CACHE, D), 0)
    lane = lax.broadcasted_iota(jnp.int32, (CACHE, D), 1)
    for j, ctx in enumerate(ctxs):
        filled = offset - ctx * CACHE
        src = msgs[j // 2]
        base = (j % 2) * SHARD

        @pl.when(filled > 0)
        def _(src=src, base=base, at=cache_rows, filled=filled):
            to = pl.ds(pl.multiple_of(at, CACHE), CACHE)
            kx[to, :D] = src[base + TOK : base + TOK + CACHE, :]
            kx[to, D:] = jnp.where((slot >= filled) & (lane == BLK), 1.0, 0.0).astype(jnp.bfloat16)
            vx[to, :] = src[base + 2 * TOK + CACHE : base + SHARD, :]

        cache_rows = cache_rows + jnp.where(filled > 0, CACHE, 0)

    ids = [table_ref[2 * ctx + b] for ctx in ctxs for b in range(2)]
    ranks = [jnp.int32(0)] * len(ids)
    for j in range(len(ids)):
        for k in range(j):
            below = (ids[k] < ids[j]).astype(jnp.int32)
            ranks[j] = ranks[j] + below
            ranks[k] = ranks[k] + 1 - below
    for j, rank in enumerate(ranks):
        to = pl.ds(pl.multiple_of(cache_rows + rank * BLK, 32), BLK)
        src = msgs[j // 4]
        base = ((j // 2) % 2) * SHARD + (j % 2) * BLK
        kx[to, :D] = src[base : base + BLK, :]
        vx[to, :] = src[base + TOK + CACHE : base + TOK + CACHE + BLK, :]

    items = jnp.int32(0)
    for qb, (g, role) in enumerate(work):
        gx, gy = g % 2, g // 2
        q_x = x + 1 - 2 * lax.rem(x, 2) if gx else x
        q_y = 1 - yl if gy else yl
        q_id = table_ref[2 * (q_x * 16 + q_y * 8 + z) + half_of[qb]]
        count = jnp.int32(0)
        own = jnp.int32(0)
        for k in ids:
            count = count + (k <= q_id).astype(jnp.int32)
            own = own + (k == q_id).astype(jnp.int32)
        end = cache_rows + count * BLK
        ends[qb] = end
        marks[qb] = jnp.where(own > 0, end - BLK, n_keys + TILE)
        tiles = (end + TILE - 1) // TILE

        def add(t, at, qb=qb):
            item_block[at] = qb
            item_tile[at] = t
            return at + 1

        items = lax.fori_loop(0, tiles, add, items)
        if first:
            m_all[qb] = jnp.full((8, ROWS), NEG, jnp.float32)
            l_all[qb] = jnp.zeros((8, ROWS), jnp.float32)
            acc_all[qb] = jnp.zeros((D, ROWS), jnp.float32)
        else:
            m_all[qb], l_all[qb] = old[3 * qb][...], old[3 * qb + 1][...]

            def bring(i, carry, qb=qb):
                rows = pl.ds(pl.multiple_of(i * 64, 64), 64)
                acc_all[qb, rows, :] = old[3 * qb + 2][rows, :]
                return carry

            lax.fori_loop(0, D // 64, bring, 0)

    pad_lane = lax.broadcasted_iota(jnp.int32, (TILE, D), 1)
    pad_rows = jnp.where(pad_lane == BLK, 1.0, 0.0).astype(jnp.bfloat16)

    def scores(s_ref, top_ref, k, before):
        old, new = item_block[before], item_block[k]
        kx[pl.ds(pl.multiple_of(ends[old], 32), TILE), D:] = jnp.zeros_like(pad_rows)
        kx[pl.ds(pl.multiple_of(marks[old], 32), BLK), D:] = jnp.zeros_like(own_rows)
        kx[pl.ds(pl.multiple_of(ends[new], 32), TILE), D:] = pad_rows
        kx[pl.ds(pl.multiple_of(marks[new], 32), BLK), D:] = own_rows
        keys = kx[pl.ds(pl.multiple_of(item_tile[k] * TILE, TILE), TILE), :]
        s = lax.dot_general(keys, qx[new], NT, preferred_element_type=jnp.float32)
        s_ref[...] = s
        top_ref[...] = jnp.broadcast_to(jnp.max(s, axis=0, keepdims=True) * SCALE, top_ref.shape)

    def absorb(s_ref, top_ref, k):
        qb = item_block[k]
        s = s_ref[...]
        m0 = m_all[qb]
        m1 = jnp.maximum(m0, top_ref[...])
        factor = jnp.exp2(m0 - m1)
        p = jnp.exp2(s * SCALE - m1[:1])
        l_all[qb] = l_all[qb] * factor + jnp.sum(p, axis=0, keepdims=True)
        m_all[qb] = m1
        values = vx[pl.ds(pl.multiple_of(item_tile[k] * TILE, TILE), TILE), :]
        acc_all[qb] = acc_all[qb] * factor[:1] + lax.dot_general(
            values, p.astype(jnp.bfloat16), TN, preferred_element_type=jnp.float32
        )

    @pl.when(items > 0)
    def _():
        scores(s_a, top_a, 0, 0)

        def pair(j, c):
            k = 2 * j
            scores(s_b, top_b, k + 1, k)
            absorb(s_a, top_a, k)
            scores(s_a, top_a, k + 2, k + 1)
            absorb(s_b, top_b, k + 1)
            return c

        lax.fori_loop(0, (items - 1) // 2, pair, 0)

        @pl.when(items % 2 == 0)
        def _():
            scores(s_b, top_b, items - 1, items - 2)
            absorb(s_a, top_a, items - 2)
            top_a[...] = top_b[...]

            def hand(i, c):
                rows = pl.ds(pl.multiple_of(i * 64, 64), 64)
                s_a[rows, :] = s_b[rows, :]
                return c

            lax.fori_loop(0, TILE // 64, hand, 0)

        absorb(s_a, top_a, items - 1)

    for qb in range(n_query):
        if last:
            total = l_all[qb]
            some = total > 0.0
            safe = jnp.where(some, total, 1.0)
            logsum = jnp.where(some, m_all[qb] + jnp.log2(safe), NEG)
            high = logsum.astype(jnp.bfloat16)
            rest = logsum - high.astype(jnp.float32)
            mid = rest.astype(jnp.bfloat16)
            low = (rest - mid.astype(jnp.float32)).astype(jnp.bfloat16)
            row = lax.broadcasted_iota(jnp.int32, (16, ROWS), 0)
            h2, m2, l2 = (jnp.concatenate([v, v], 0).astype(jnp.float32) for v in (high, mid, low))
            outs[qb][:D, :] = (acc_all[qb] / safe[:1]).astype(jnp.bfloat16)
            outs[qb][D:, :] = jnp.where(row == 0, h2, jnp.where(row == 1, m2, l2)).astype(jnp.bfloat16)
        else:
            outs[3 * qb][...], outs[3 * qb + 1][...] = m_all[qb], l_all[qb]

            def keep(i, carry, qb=qb):
                rows = pl.ds(pl.multiple_of(i * 64, 64), 64)
                outs[3 * qb + 2][rows, :] = acc_all[qb, rows, :]
                return carry

            lax.fori_loop(0, D // 64, keep, 0)


def run_chunk(work, steps, state, last, table, queries, messages):
    first = work[0] not in state
    sets = sorted({g for g, _ in work})
    n_query = len(work)
    n_keys = 256 * 2 * len(steps)
    keep = n_keys + TILE + 128
    max_items = n_query * (n_keys // TILE + 1) + 2
    shapes = [(8, ROWS), (8, ROWS), (D, ROWS)]
    smem = pl.BlockSpec(memory_space=pltpu.SMEM)
    vmem = pl.BlockSpec(memory_space=VMEM)
    operands = [table, *(queries[g] for g in sets), *messages]
    if not first:
        operands += [array for key in work for array in state[key]]
    if last:
        out_shape = [jax.ShapeDtypeStruct((OUT_ROWS, ROWS), jnp.bfloat16)] * n_query
    else:
        out_shape = [jax.ShapeDtypeStruct(s, jnp.float32) for s in shapes] * n_query
    pairs = n_query * n_keys * ROWS * 6 // 10
    name = "_".join(["attend", *(str(g) + "AB"[role] for g, role in work), str(len(steps))])
    results = pl.pallas_call(
        functools.partial(attend_chunk, tuple(work), tuple(sets), tuple(steps), first, last),
        out_shape=out_shape,
        in_specs=[smem] + [vmem] * (len(operands) - 1),
        out_specs=[vmem] * len(out_shape),
        scratch_shapes=[VMEM((n_query, *s), jnp.float32) for s in shapes]
        + [
            VMEM((n_query, ROWS, 2 * D), jnp.bfloat16),
            VMEM((keep, 2 * D), jnp.bfloat16),
            VMEM((keep, D), jnp.bfloat16),
            VMEM((TILE, ROWS), jnp.float32),
            VMEM((TILE, ROWS), jnp.float32),
            VMEM((8, ROWS), jnp.float32),
            VMEM((8, ROWS), jnp.float32),
            pltpu.SMEM((8,), jnp.int32),
            pltpu.SMEM((8,), jnp.int32),
            pltpu.SMEM((max_items,), jnp.int32),
            pltpu.SMEM((max_items,), jnp.int32),
        ],
        compiler_params=pltpu.CompilerParams(vmem_limit_bytes=24 * 2**20),
        cost_estimate=pl.CostEstimate(
            flops=1024 if sets == [0] else pairs * 1024, bytes_accessed=1024 if sets == [0] else 8 * 2**20, transcendentals=0
        ),
        name=name,
    )(*operands)
    if last:
        return results
    for i, key in enumerate(work):
        state[key] = tuple(results[3 * i : 3 * i + 3])
    return state


def project_body(table_ref, a_ref, b_ref, c_ref, d_ref, w_ref, give_ref, mine_ref, att):
    parts = (a_ref, b_ref, c_ref, d_ref)
    logs = []
    for part in parts:
        row = part[D:, :].astype(jnp.float32)
        logs.append(row[0:1] + row[1:2] + row[2:3])
    top = functools.reduce(jnp.maximum, logs)
    weights = [jnp.exp2(v - top) for v in logs]
    share = 1.0 / sum(weights)
    mixed = sum(part[:D, :].astype(jnp.float32) * (w * share) for part, w in zip(parts, weights))
    turned = mixed.T.astype(jnp.bfloat16)
    for h in range(HEADS):
        att[:, h * D : (h + 1) * D] = turned[h * BLK : (h + 1) * BLK, :]
    core = table_ref[PLACE + 4]
    half = BLK // 2
    wide = 2048

    def columns(c, carry):
        cols = pl.ds(pl.multiple_of(c * wide, wide), wide)
        full = jnp.dot(att[...], w_ref[:, cols], preferred_element_type=jnp.float32)
        give_ref[:, cols] = jnp.where(core == 0, full[half:], full[:half]).astype(jnp.bfloat16)
        mine_ref[:, cols] = jnp.where(core == 0, full[:half], full[half:])
        return carry

    lax.fori_loop(0, w_ref.shape[1] // wide, columns, 0)


def project(table, parts, weight):
    vmem = pl.BlockSpec(memory_space=VMEM)
    wide = weight.shape[1]
    return pl.pallas_call(
        project_body,
        out_shape=(
            jax.ShapeDtypeStruct((BLK // 2, wide), jnp.bfloat16),
            jax.ShapeDtypeStruct((BLK // 2, wide), jnp.float32),
        ),
        in_specs=[pl.BlockSpec(memory_space=pltpu.SMEM)] + [vmem] * 5,
        out_specs=(vmem, vmem),
        scratch_shapes=[VMEM((BLK, HEADS * D), jnp.bfloat16)],
        compiler_params=pltpu.CompilerParams(vmem_limit_bytes=24 * 2**20),
        cost_estimate=pl.CostEstimate(flops=2 * BLK * HEADS * D * wide, bytes_accessed=12 * 2**20, transcendentals=0),
        name="project",
    )(table, *parts, weight)


def total_body(a_ref, b_ref, out):
    out[...] = (a_ref[...].astype(jnp.float32) + b_ref[...].astype(jnp.float32)).astype(out.dtype)


def total(a, b, dtype):
    vmem = pl.BlockSpec(memory_space=VMEM)
    return pl.pallas_call(
        total_body,
        out_shape=jax.ShapeDtypeStruct(a.shape, dtype),
        in_specs=[vmem] * 2,
        out_specs=vmem,
        compiler_params=pltpu.CompilerParams(vmem_limit_bytes=8 * 2**20),
        name="total",
    )(a, b)


def stage_body(src, dst):
    dst[...] = src[...]


def stage(array):
    vmem = pl.BlockSpec(memory_space=VMEM)
    return pl.pallas_call(
        stage_body,
        out_shape=jax.ShapeDtypeStruct(array.shape, array.dtype),
        in_specs=[vmem],
        out_specs=vmem,
        compiler_params=pltpu.CompilerParams(vmem_limit_bytes=8 * 2**20),
        name="stage",
    )(array)


def on_device(queries, window_keys, window_values, stored_keys, stored_values, block_order, window_offset, out_weight):
    x, yl, z = lax.axis_index("x"), lax.axis_index("yl"), lax.axis_index("z")
    core, yh = lax.axis_index("core"), lax.axis_index("yh")
    place = jnp.stack([x, yl, z, window_offset[0], core, yh]).astype(jnp.int32)
    table = jnp.concatenate([block_order, place])
    shard = jnp.concatenate([window_keys, stored_keys, window_values, stored_values], 0)

    def along(array, axis, size, to):
        return lax.ppermute(array, axis, [(i, to(i)) for i in range(size)])

    shard, queries = lax.optimization_barrier((shard, queries))
    other = along(shard, "x", 4, lambda i: 3 - i)
    base = jnp.concatenate([shard, other], 0)
    pair = [(a, b) for a in range(4) for b in range(2)]
    both = [(2 * a + b, 2 * (a ^ 1) + (1 - b)) for a, b in pair]
    to_member = [
        lambda v: v,
        lambda v: along(v, "x", 4, lambda i: i ^ 1),
        lambda v: along(v, "yl", 2, lambda i: 1 - i),
        lambda v: lax.ppermute(v, ("x", "yl"), both),
    ]
    q_sets = [queries] + [to_member[g](queries) for g in (1, 2, 3)]
    up = lambda a: along(a, "z", 8, lambda i: (i + 1) % 8)
    down = lambda a: along(a, "z", 8, lambda i: (i - 1) % 8)
    base, table, q_sets[0] = lax.optimization_barrier((base, table, stage(queries)))
    a1, b1 = up(base), down(base)
    a2, b2 = up(a1), down(b1)
    state = {}
    run = lambda work, steps, messages, last=False: run_chunk(work, steps, state, last, table, q_sets, messages)
    tie = lax.optimization_barrier
    near = (0, -1, 1), (base, a1, b1)
    A, B = 0, 1
    run([(0, A), (0, B)], *near)
    run([(3, A), (3, B)], *near)
    a2, b2, state[0, A], state[3, A] = tie((a2, b2, state[0, A], state[3, A]))
    a3, b3 = up(a2), down(b2)
    far = jnp.concatenate([up(a3[:SHARD]), down(b3[SHARD:])], 0)
    run([(1, A), (1, B), (2, A), (2, B)], *near)
    run([(g, r) for r in (A, B) for g in (1, 2, 3)], (-2, 2), (a2, b2))
    end = (-3, 3, 4), (a3, b3, far)
    sent_a = run([(3, A), (1, A), (2, A)], *end, True)
    *sent_a, state[3, B] = tie((*sent_a, state[3, B]))
    got_a = [to_member[g](v) for g, v in zip((3, 1, 2), sent_a)]
    sent_b = run([(3, B), (1, B), (2, B)], *end, True)
    *sent_b, state[0, A] = tie((*sent_b, state[0, A]))
    got_b = [to_member[g](v) for g, v in zip((3, 1, 2), sent_b)]
    rest = (-2, 2, -3, 3, 4), (a2, b2, a3, b3, far)
    (own_a,) = run([(0, A)], *rest, True)
    swap = lambda v, axis: along(v, axis, 2, lambda i: 1 - i)
    give_a, keep_a = project(table, (own_a, *got_a), out_weight)
    give_a, *got_b = tie((give_a, *got_b))
    sum_a = total(keep_a, swap(give_a, "core"), jnp.bfloat16)
    sum_a, state[0, B] = tie((sum_a, state[0, B]))
    across = swap(sum_a, "yh")
    (own_b,) = run([(0, B)], *rest, True)
    give_b, keep_b = project(table, (own_b, *got_b), out_weight)
    keep_b = total(keep_b, across, jnp.float32)
    return (keep_b + swap(give_b, "core").astype(jnp.float32)).astype(jnp.bfloat16)


def solution(mesh):
    fine = Mesh(mesh.devices.reshape(4, 2, 8, 2, 2), ("x", "yl", "z", "yh", "core"))
    ctx, tp = ("x", "yl", "z"), ("yh", "core")
    return jax.shard_map(
        on_device,
        mesh=fine,
        in_specs=(P(ctx, tp),) * 5 + (P(), P(), P(tp, None)),
        out_specs=P((*ctx, *tp), None),
        check_vma=False,
    )
```

```python
import functools

import jax
import jax.numpy as jnp
from jax import lax
from jax.experimental import pallas as pl
from jax.experimental.pallas import tpu as pltpu
from jax.sharding import Mesh, PartitionSpec as P

HEADS = 8
D = 128
BLK = 96
TOK = 2 * BLK
CACHE = 64
SHARD = 2 * (TOK + CACHE)
ROWS = HEADS * BLK
TILE = 384
NEG = -1e30
SCALE = D**-0.5 * 1.4426950408889634
PLACE = 128
OUT_ROWS = D + 16
NT = (((1,), (1,)), ((), ()))
TN = (((0,), (0,)), ((), ()))
VMEM = pltpu.VMEM


def attend_chunk(work, sets, steps, first, last, *refs):
    refs = list(refs)

    def take(count):
        taken = refs[:count]
        del refs[:count]
        return taken

    n_query = len(work)
    (table_ref,) = take(1)
    q_refs = take(len(sets))
    msgs = take(len(steps))
    old = [] if first else take(3 * n_query)
    outs = take(n_query if last else 3 * n_query)
    m_all, l_all, acc_all, qx, kx, vx, s_a, s_b, top_a, top_b, ends, marks, item_block, item_tile = refs
    x, yl, z, offset, yh = (table_ref[PLACE + i] for i in (0, 1, 2, 3, 5))
    n_keys = 256 * 2 * len(steps)

    token = lax.broadcasted_iota(jnp.int32, (BLK, D), 0)
    column = lax.broadcasted_iota(jnp.int32, (BLK, D), 1)
    hidden = ((column < BLK) & (column > token)) | (column == BLK)
    q_extra = jnp.where(hidden, NEG, 0.0).astype(jnp.bfloat16)
    own_rows = jnp.where(column == token, 1.0, 0.0).astype(jnp.bfloat16)
    half_of = [yh if role else 1 - yh for _, role in work]
    for qb, (g, role) in enumerate(work):
        src = q_refs[sets.index(g)]
        at = pl.ds(pl.multiple_of(half_of[qb] * BLK, 32), BLK)

        def stage_head(h, carry, qb=qb, src=src, at=at):
            rows = pl.ds(pl.multiple_of(h * BLK, 32), BLK)
            qx[qb, rows, :D] = src[at, pl.ds(pl.multiple_of(h * D, D), D)]
            qx[qb, rows, D:] = q_extra
            return carry

        lax.fori_loop(0, HEADS, stage_head, 0, unroll=2)

    def clear_marks(i, carry):
        rows = pl.ds(pl.multiple_of(i * D, D), D)
        kx[rows, D:] = jnp.zeros((D, D), jnp.bfloat16)
        return carry

    def clear_tail(i, carry):
        rows = pl.ds(pl.multiple_of(i * D, D), D)
        kx[rows, :D] = jnp.zeros((D, D), jnp.bfloat16)
        vx[rows, :] = jnp.zeros((D, D), jnp.bfloat16)
        return carry

    lax.fori_loop(0, kx.shape[0] // D, clear_marks, 0)
    lax.fori_loop(n_keys // D - len(steps), kx.shape[0] // D, clear_tail, 0)

    ctxs = []
    for step in steps:
        zz = lax.rem(z + step + 8, 8)
        ctxs += [x * 16 + yl * 8 + zz, (3 - x) * 16 + yl * 8 + zz]
    cache_rows = jnp.int32(0)
    slot = lax.broadcasted_iota(jnp.int32, (CACHE, D), 0)
    lane = lax.broadcasted_iota(jnp.int32, (CACHE, D), 1)
    for j, ctx in enumerate(ctxs):
        filled = offset - ctx * CACHE
        src = msgs[j // 2]
        base = (j % 2) * SHARD

        @pl.when(filled > 0)
        def _(src=src, base=base, at=cache_rows, filled=filled):
            to = pl.ds(pl.multiple_of(at, CACHE), CACHE)
            kx[to, :D] = src[base + TOK : base + TOK + CACHE, :]
            kx[to, D:] = jnp.where((slot >= filled) & (lane == BLK), 1.0, 0.0).astype(jnp.bfloat16)
            vx[to, :] = src[base + 2 * TOK + CACHE : base + SHARD, :]

        cache_rows = cache_rows + jnp.where(filled > 0, CACHE, 0)

    ids = [table_ref[2 * ctx + b] for ctx in ctxs for b in range(2)]
    ranks = [jnp.int32(0)] * len(ids)
    for j in range(len(ids)):
        for k in range(j):
            below = (ids[k] < ids[j]).astype(jnp.int32)
            ranks[j] = ranks[j] + below
            ranks[k] = ranks[k] + 1 - below
    for j, rank in enumerate(ranks):
        to = pl.ds(pl.multiple_of(cache_rows + rank * BLK, 32), BLK)
        src = msgs[j // 4]
        base = ((j // 2) % 2) * SHARD + (j % 2) * BLK
        kx[to, :D] = src[base : base + BLK, :]
        vx[to, :] = src[base + TOK + CACHE : base + TOK + CACHE + BLK, :]

    items = jnp.int32(0)
    for qb, (g, role) in enumerate(work):
        gx, gy = g % 2, g // 2
        q_x = x + 1 - 2 * lax.rem(x, 2) if gx else x
        q_y = 1 - yl if gy else yl
        q_id = table_ref[2 * (q_x * 16 + q_y * 8 + z) + half_of[qb]]
        count = jnp.int32(0)
        own = jnp.int32(0)
        for k in ids:
            count = count + (k <= q_id).astype(jnp.int32)
            own = own + (k == q_id).astype(jnp.int32)
        end = cache_rows + count * BLK
        ends[qb] = end
        marks[qb] = jnp.where(own > 0, end - BLK, n_keys + TILE)
        tiles = (end + TILE - 1) // TILE

        def add(t, at, qb=qb):
            item_block[at] = qb
            item_tile[at] = t
            return at + 1

        items = lax.fori_loop(0, tiles, add, items)
        if first:
            m_all[qb] = jnp.full((8, ROWS), NEG, jnp.float32)
            l_all[qb] = jnp.zeros((8, ROWS), jnp.float32)
            acc_all[qb] = jnp.zeros((D, ROWS), jnp.float32)
        else:
            m_all[qb], l_all[qb] = old[3 * qb][...], old[3 * qb + 1][...]

            def bring(i, carry, qb=qb):
                rows = pl.ds(pl.multiple_of(i * 64, 64), 64)
                acc_all[qb, rows, :] = old[3 * qb + 2][rows, :]
                return carry

            lax.fori_loop(0, D // 64, bring, 0)

    pad_lane = lax.broadcasted_iota(jnp.int32, (TILE, D), 1)
    pad_rows = jnp.where(pad_lane == BLK, 1.0, 0.0).astype(jnp.bfloat16)

    def scores(s_ref, top_ref, k, before):
        old, new = item_block[before], item_block[k]
        kx[pl.ds(pl.multiple_of(ends[old], 32), TILE), D:] = jnp.zeros_like(pad_rows)
        kx[pl.ds(pl.multiple_of(marks[old], 32), BLK), D:] = jnp.zeros_like(own_rows)
        kx[pl.ds(pl.multiple_of(ends[new], 32), TILE), D:] = pad_rows
        kx[pl.ds(pl.multiple_of(marks[new], 32), BLK), D:] = own_rows
        keys = kx[pl.ds(pl.multiple_of(item_tile[k] * TILE, TILE), TILE), :]
        s = lax.dot_general(keys, qx[new], NT, preferred_element_type=jnp.float32)
        s_ref[...] = s
        top_ref[...] = jnp.broadcast_to(jnp.max(s, axis=0, keepdims=True) * SCALE, top_ref.shape)

    def absorb(s_ref, top_ref, k):
        qb = item_block[k]
        s = s_ref[...]
        m0 = m_all[qb]
        m1 = jnp.maximum(m0, top_ref[...])
        factor = jnp.exp2(m0 - m1)
        p = jnp.exp2(s * SCALE - m1[:1])
        l_all[qb] = l_all[qb] * factor + jnp.sum(p, axis=0, keepdims=True)
        m_all[qb] = m1
        values = vx[pl.ds(pl.multiple_of(item_tile[k] * TILE, TILE), TILE), :]
        acc_all[qb] = acc_all[qb] * factor[:1] + lax.dot_general(
            values, p.astype(jnp.bfloat16), TN, preferred_element_type=jnp.float32
        )

    @pl.when(items > 0)
    def _():
        scores(s_a, top_a, 0, 0)

        def pair(j, c):
            k = 2 * j
            scores(s_b, top_b, k + 1, k)
            absorb(s_a, top_a, k)
            scores(s_a, top_a, k + 2, k + 1)
            absorb(s_b, top_b, k + 1)
            return c

        lax.fori_loop(0, (items - 1) // 2, pair, 0)

        @pl.when(items % 2 == 0)
        def _():
            scores(s_b, top_b, items - 1, items - 2)
            absorb(s_a, top_a, items - 2)
            top_a[...] = top_b[...]

            def hand(i, c):
                rows = pl.ds(pl.multiple_of(i * 64, 64), 64)
                s_a[rows, :] = s_b[rows, :]
                return c

            lax.fori_loop(0, TILE // 64, hand, 0)

        absorb(s_a, top_a, items - 1)

    for qb in range(n_query):
        if last:
            total = l_all[qb]
            some = total > 0.0
            safe = jnp.where(some, total, 1.0)
            logsum = jnp.where(some, m_all[qb] + jnp.log2(safe), NEG)
            high = logsum.astype(jnp.bfloat16)
            rest = logsum - high.astype(jnp.float32)
            mid = rest.astype(jnp.bfloat16)
            low = (rest - mid.astype(jnp.float32)).astype(jnp.bfloat16)
            row = lax.broadcasted_iota(jnp.int32, (16, ROWS), 0)
            h2, m2, l2 = (jnp.concatenate([v, v], 0).astype(jnp.float32) for v in (high, mid, low))
            outs[qb][:D, :] = (acc_all[qb] / safe[:1]).astype(jnp.bfloat16)
            outs[qb][D:, :] = jnp.where(row == 0, h2, jnp.where(row == 1, m2, l2)).astype(jnp.bfloat16)
        else:
            outs[3 * qb][...], outs[3 * qb + 1][...] = m_all[qb], l_all[qb]

            def keep(i, carry, qb=qb):
                rows = pl.ds(pl.multiple_of(i * 64, 64), 64)
                outs[3 * qb + 2][rows, :] = acc_all[qb, rows, :]
                return carry

            lax.fori_loop(0, D // 64, keep, 0)


def run_chunk(work, steps, state, last, table, queries, messages):
    first = work[0] not in state
    sets = sorted({g for g, _ in work})
    n_query = len(work)
    n_keys = 256 * 2 * len(steps)
    keep = n_keys + TILE + 128
    max_items = n_query * (n_keys // TILE + 1) + 2
    shapes = [(8, ROWS), (8, ROWS), (D, ROWS)]
    smem = pl.BlockSpec(memory_space=pltpu.SMEM)
    vmem = pl.BlockSpec(memory_space=VMEM)
    operands = [table, *(queries[g] for g in sets), *messages]
    if not first:
        operands += [array for key in work for array in state[key]]
    if last:
        out_shape = [jax.ShapeDtypeStruct((OUT_ROWS, ROWS), jnp.bfloat16)] * n_query
    else:
        out_shape = [jax.ShapeDtypeStruct(s, jnp.float32) for s in shapes] * n_query
    pairs = n_query * n_keys * ROWS * 6 // 10
    name = "_".join(["attend", *(str(g) + "AB"[role] for g, role in work), str(len(steps))])
    results = pl.pallas_call(
        functools.partial(attend_chunk, tuple(work), tuple(sets), tuple(steps), first, last),
        out_shape=out_shape,
        in_specs=[smem] + [vmem] * (len(operands) - 1),
        out_specs=[vmem] * len(out_shape),
        scratch_shapes=[VMEM((n_query, *s), jnp.float32) for s in shapes]
        + [
            VMEM((n_query, ROWS, 2 * D), jnp.bfloat16),
            VMEM((keep, 2 * D), jnp.bfloat16),
            VMEM((keep, D), jnp.bfloat16),
            VMEM((TILE, ROWS), jnp.float32),
            VMEM((TILE, ROWS), jnp.float32),
            VMEM((8, ROWS), jnp.float32),
            VMEM((8, ROWS), jnp.float32),
            pltpu.SMEM((8,), jnp.int32),
            pltpu.SMEM((8,), jnp.int32),
            pltpu.SMEM((max_items,), jnp.int32),
            pltpu.SMEM((max_items,), jnp.int32),
        ],
        compiler_params=pltpu.CompilerParams(vmem_limit_bytes=24 * 2**20),
        cost_estimate=pl.CostEstimate(
            flops=1024 if sets == [0] else pairs * 1024, bytes_accessed=1024 if sets == [0] else 8 * 2**20, transcendentals=0
        ),
        name=name,
    )(*operands)
    if last:
        return results
    for i, key in enumerate(work):
        state[key] = tuple(results[3 * i : 3 * i + 3])
    return state


def project_body(table_ref, a_ref, b_ref, c_ref, d_ref, w_ref, give_ref, mine_ref, att):
    parts = (a_ref, b_ref, c_ref, d_ref)
    logs = []
    for part in parts:
        row = part[D:, :].astype(jnp.float32)
        logs.append(row[0:1] + row[1:2] + row[2:3])
    top = functools.reduce(jnp.maximum, logs)
    weights = [jnp.exp2(v - top) for v in logs]
    share = 1.0 / sum(weights)
    mixed = sum(part[:D, :].astype(jnp.float32) * (w * share) for part, w in zip(parts, weights))
    turned = mixed.T.astype(jnp.bfloat16)
    for h in range(HEADS):
        att[:, h * D : (h + 1) * D] = turned[h * BLK : (h + 1) * BLK, :]
    core = table_ref[PLACE + 4]
    half = BLK // 2
    wide = 1024

    def columns(c, carry):
        cols = pl.ds(pl.multiple_of(c * wide, wide), wide)
        full = jnp.dot(att[...], w_ref[:, cols], preferred_element_type=jnp.float32)
        give_ref[:, cols] = jnp.where(core == 0, full[half:], full[:half]).astype(jnp.bfloat16)
        mine_ref[:, cols] = jnp.where(core == 0, full[:half], full[half:])
        return carry

    lax.fori_loop(0, w_ref.shape[1] // wide, columns, 0)


def project(table, parts, weight):
    vmem = pl.BlockSpec(memory_space=VMEM)
    wide = weight.shape[1]
    return pl.pallas_call(
        project_body,
        out_shape=(
            jax.ShapeDtypeStruct((BLK // 2, wide), jnp.bfloat16),
            jax.ShapeDtypeStruct((BLK // 2, wide), jnp.float32),
        ),
        in_specs=[pl.BlockSpec(memory_space=pltpu.SMEM)] + [vmem] * 5,
        out_specs=(vmem, vmem),
        scratch_shapes=[VMEM((BLK, HEADS * D), jnp.bfloat16)],
        compiler_params=pltpu.CompilerParams(vmem_limit_bytes=24 * 2**20),
        cost_estimate=pl.CostEstimate(flops=2 * BLK * HEADS * D * wide, bytes_accessed=12 * 2**20, transcendentals=0),
        name="project",
    )(table, *parts, weight)


def total_body(a_ref, b_ref, out):
    out[...] = (a_ref[...].astype(jnp.float32) + b_ref[...].astype(jnp.float32)).astype(out.dtype)


def total(a, b, dtype):
    vmem = pl.BlockSpec(memory_space=VMEM)
    return pl.pallas_call(
        total_body,
        out_shape=jax.ShapeDtypeStruct(a.shape, dtype),
        in_specs=[vmem] * 2,
        out_specs=vmem,
        compiler_params=pltpu.CompilerParams(vmem_limit_bytes=8 * 2**20),
        name="total",
    )(a, b)


def stage_body(src, dst):
    dst[...] = src[...]


def stage(array):
    vmem = pl.BlockSpec(memory_space=VMEM)
    return pl.pallas_call(
        stage_body,
        out_shape=jax.ShapeDtypeStruct(array.shape, array.dtype),
        in_specs=[vmem],
        out_specs=vmem,
        compiler_params=pltpu.CompilerParams(vmem_limit_bytes=8 * 2**20),
        name="stage",
    )(array)


def on_device(queries, window_keys, window_values, stored_keys, stored_values, block_order, window_offset, out_weight):
    x, yl, z = lax.axis_index("x"), lax.axis_index("yl"), lax.axis_index("z")
    core, yh = lax.axis_index("core"), lax.axis_index("yh")
    place = jnp.stack([x, yl, z, window_offset[0], core, yh]).astype(jnp.int32)
    table = jnp.concatenate([block_order, place])
    shard = jnp.concatenate([window_keys, stored_keys, window_values, stored_values], 0)

    def along(array, axis, size, to):
        return lax.ppermute(array, axis, [(i, to(i)) for i in range(size)])

    shard, queries = lax.optimization_barrier((shard, queries))
    other = along(shard, "x", 4, lambda i: 3 - i)
    base = jnp.concatenate([shard, other], 0)
    pair = [(a, b) for a in range(4) for b in range(2)]
    both = [(2 * a + b, 2 * (a ^ 1) + (1 - b)) for a, b in pair]
    to_member = [
        lambda v: v,
        lambda v: along(v, "x", 4, lambda i: i ^ 1),
        lambda v: along(v, "yl", 2, lambda i: 1 - i),
        lambda v: lax.ppermute(v, ("x", "yl"), both),
    ]
    q_sets = [queries] + [to_member[g](queries) for g in (1, 2, 3)]
    up = lambda a: along(a, "z", 8, lambda i: (i + 1) % 8)
    down = lambda a: along(a, "z", 8, lambda i: (i - 1) % 8)
    base, table, q_sets[0] = lax.optimization_barrier((base, table, stage(queries)))
    a1, b1 = up(base), down(base)
    a2, b2 = up(a1), down(b1)
    state = {}
    run = lambda work, steps, messages, last=False: run_chunk(work, steps, state, last, table, q_sets, messages)
    tie = lax.optimization_barrier
    near = (0, -1, 1), (base, a1, b1)
    A, B = 0, 1
    run([(0, A), (0, B)], *near)
    run([(3, A), (3, B)], *near)
    a2, b2, state[0, A], state[3, A] = tie((a2, b2, state[0, A], state[3, A]))
    a3, b3 = up(a2), down(b2)
    far = jnp.concatenate([up(a3[:SHARD]), down(b3[SHARD:])], 0)
    run([(1, A), (1, B), (2, A), (2, B)], *near)
    run([(g, r) for r in (A, B) for g in (1, 2, 3)], (-2, 2), (a2, b2))
    end = (-3, 3, 4), (a3, b3, far)
    sent_a = run([(3, A), (1, A), (2, A)], *end, True)
    *sent_a, state[3, B] = tie((*sent_a, state[3, B]))
    got_a = [to_member[g](v) for g, v in zip((3, 1, 2), sent_a)]
    sent_b = run([(3, B), (1, B), (2, B)], *end, True)
    *sent_b, state[0, A] = tie((*sent_b, state[0, A]))
    got_b = [to_member[g](v) for g, v in zip((3, 1, 2), sent_b)]
    rest = (-2, 2, -3, 3, 4), (a2, b2, a3, b3, far)
    (own_a,) = run([(0, A)], *rest, True)
    swap = lambda v, axis: along(v, axis, 2, lambda i: 1 - i)
    give_a, keep_a = project(table, (own_a, *got_a), out_weight)
    give_a, *got_b = tie((give_a, *got_b))
    sum_a = total(keep_a, swap(give_a, "core"), jnp.bfloat16)
    sum_a, state[0, B] = tie((sum_a, state[0, B]))
    across = swap(sum_a, "yh")
    (own_b,) = run([(0, B)], *rest, True)
    give_b, keep_b = project(table, (own_b, *got_b), out_weight)
    keep_b = total(keep_b, across, jnp.float32)
    return (keep_b + swap(give_b, "core").astype(jnp.float32)).astype(jnp.bfloat16)


def solution(mesh):
    fine = Mesh(mesh.devices.reshape(4, 2, 8, 2, 2), ("x", "yl", "z", "yh", "core"))
    ctx, tp = ("x", "yl", "z"), ("yh", "core")
    return jax.shard_map(
        on_device,
        mesh=fine,
        in_specs=(P(ctx, tp),) * 5 + (P(), P(), P(tp, None)),
        out_specs=P((*ctx, *tp), None),
        check_vma=False,
    )
```

```python
import functools

import jax
import jax.numpy as jnp
from jax import lax
from jax.experimental import pallas as pl
from jax.experimental.pallas import tpu as pltpu
from jax.sharding import Mesh, PartitionSpec as P

HEADS = 8
D = 128
BLK = 96
TOK = 2 * BLK
CACHE = 64
SHARD = 2 * (TOK + CACHE)
ROWS = HEADS * BLK
TILE = 384
NEG = -1e30
SCALE = D**-0.5 * 1.4426950408889634
PLACE = 128
OUT_ROWS = D + 16
NT = (((1,), (1,)), ((), ()))
TN = (((0,), (0,)), ((), ()))
VMEM = pltpu.VMEM


def attend_chunk(work, sets, steps, first, last, *refs):
    refs = list(refs)

    def take(count):
        taken = refs[:count]
        del refs[:count]
        return taken

    n_query = len(work)
    (table_ref,) = take(1)
    q_refs = take(len(sets))
    msgs = take(len(steps))
    old = [] if first else take(3 * n_query)
    outs = take(n_query if last else 3 * n_query)
    m_all, l_all, acc_all, qx, kx, vx, s_a, s_b, top_a, top_b, ends, marks, item_block, item_tile = refs
    x, yl, z, offset, yh = (table_ref[PLACE + i] for i in (0, 1, 2, 3, 5))
    n_keys = 256 * 2 * len(steps)

    token = lax.broadcasted_iota(jnp.int32, (BLK, D), 0)
    column = lax.broadcasted_iota(jnp.int32, (BLK, D), 1)
    hidden = ((column < BLK) & (column > token)) | (column == BLK)
    q_extra = jnp.where(hidden, NEG, 0.0).astype(jnp.bfloat16)
    own_rows = jnp.where(column == token, 1.0, 0.0).astype(jnp.bfloat16)
    half_of = [yh if role else 1 - yh for _, role in work]
    for qb, (g, role) in enumerate(work):
        src = q_refs[sets.index(g)]
        at = pl.ds(pl.multiple_of(half_of[qb] * BLK, 32), BLK)

        def stage_head(h, carry, qb=qb, src=src, at=at):
            rows = pl.ds(pl.multiple_of(h * BLK, 32), BLK)
            qx[qb, rows, :D] = src[at, pl.ds(pl.multiple_of(h * D, D), D)]
            qx[qb, rows, D:] = q_extra
            return carry

        lax.fori_loop(0, HEADS, stage_head, 0, unroll=4)

    def clear_marks(i, carry):
        rows = pl.ds(pl.multiple_of(i * D, D), D)
        kx[rows, D:] = jnp.zeros((D, D), jnp.bfloat16)
        return carry

    def clear_tail(i, carry):
        rows = pl.ds(pl.multiple_of(i * D, D), D)
        kx[rows, :D] = jnp.zeros((D, D), jnp.bfloat16)
        vx[rows, :] = jnp.zeros((D, D), jnp.bfloat16)
        return carry

    lax.fori_loop(0, kx.shape[0] // D, clear_marks, 0)
    lax.fori_loop(n_keys // D - len(steps), kx.shape[0] // D, clear_tail, 0)

    ctxs = []
    for step in steps:
        zz = lax.rem(z + step + 8, 8)
        ctxs += [x * 16 + yl * 8 + zz, (3 - x) * 16 + yl * 8 + zz]
    cache_rows = jnp.int32(0)
    slot = lax.broadcasted_iota(jnp.int32, (CACHE, D), 0)
    lane = lax.broadcasted_iota(jnp.int32, (CACHE, D), 1)
    for j, ctx in enumerate(ctxs):
        filled = offset - ctx * CACHE
        src = msgs[j // 2]
        base = (j % 2) * SHARD

        @pl.when(filled > 0)
        def _(src=src, base=base, at=cache_rows, filled=filled):
            to = pl.ds(pl.multiple_of(at, CACHE), CACHE)
            kx[to, :D] = src[base + TOK : base + TOK + CACHE, :]
            kx[to, D:] = jnp.where((slot >= filled) & (lane == BLK), 1.0, 0.0).astype(jnp.bfloat16)
            vx[to, :] = src[base + 2 * TOK + CACHE : base + SHARD, :]

        cache_rows = cache_rows + jnp.where(filled > 0, CACHE, 0)

    ids = [table_ref[2 * ctx + b] for ctx in ctxs for b in range(2)]
    ranks = [jnp.int32(0)] * len(ids)
    for j in range(len(ids)):
        for k in range(j):
            below = (ids[k] < ids[j]).astype(jnp.int32)
            ranks[j] = ranks[j] + below
            ranks[k] = ranks[k] + 1 - below
    for j, rank in enumerate(ranks):
        to = pl.ds(pl.multiple_of(cache_rows + rank * BLK, 32), BLK)
        src = msgs[j // 4]
        base = ((j // 2) % 2) * SHARD + (j % 2) * BLK
        kx[to, :D] = src[base : base + BLK, :]
        vx[to, :] = src[base + TOK + CACHE : base + TOK + CACHE + BLK, :]

    items = jnp.int32(0)
    for qb, (g, role) in enumerate(work):
        gx, gy = g % 2, g // 2
        q_x = x + 1 - 2 * lax.rem(x, 2) if gx else x
        q_y = 1 - yl if gy else yl
        q_id = table_ref[2 * (q_x * 16 + q_y * 8 + z) + half_of[qb]]
        count = jnp.int32(0)
        own = jnp.int32(0)
        for k in ids:
            count = count + (k <= q_id).astype(jnp.int32)
            own = own + (k == q_id).astype(jnp.int32)
        end = cache_rows + count * BLK
        ends[qb] = end
        marks[qb] = jnp.where(own > 0, end - BLK, n_keys + TILE)
        tiles = (end + TILE - 1) // TILE

        def add(t, at, qb=qb):
            item_block[at] = qb
            item_tile[at] = t
            return at + 1

        items = lax.fori_loop(0, tiles, add, items)
        if first:
            m_all[qb] = jnp.full((8, ROWS), NEG, jnp.float32)
            l_all[qb] = jnp.zeros((8, ROWS), jnp.float32)
            acc_all[qb] = jnp.zeros((D, ROWS), jnp.float32)
        else:
            m_all[qb], l_all[qb] = old[3 * qb][...], old[3 * qb + 1][...]

            def bring(i, carry, qb=qb):
                rows = pl.ds(pl.multiple_of(i * 64, 64), 64)
                acc_all[qb, rows, :] = old[3 * qb + 2][rows, :]
                return carry

            lax.fori_loop(0, D // 64, bring, 0)

    pad_lane = lax.broadcasted_iota(jnp.int32, (TILE, D), 1)
    pad_rows = jnp.where(pad_lane == BLK, 1.0, 0.0).astype(jnp.bfloat16)

    def scores(s_ref, top_ref, k, before):
        old, new = item_block[before], item_block[k]
        kx[pl.ds(pl.multiple_of(ends[old], 32), TILE), D:] = jnp.zeros_like(pad_rows)
        kx[pl.ds(pl.multiple_of(marks[old], 32), BLK), D:] = jnp.zeros_like(own_rows)
        kx[pl.ds(pl.multiple_of(ends[new], 32), TILE), D:] = pad_rows
        kx[pl.ds(pl.multiple_of(marks[new], 32), BLK), D:] = own_rows
        keys = kx[pl.ds(pl.multiple_of(item_tile[k] * TILE, TILE), TILE), :]
        s = lax.dot_general(keys, qx[new], NT, preferred_element_type=jnp.float32)
        s_ref[...] = s
        top_ref[...] = jnp.broadcast_to(jnp.max(s, axis=0, keepdims=True) * SCALE, top_ref.shape)

    def absorb(s_ref, top_ref, k):
        qb = item_block[k]
        s = s_ref[...]
        m0 = m_all[qb]
        m1 = jnp.maximum(m0, top_ref[...])
        factor = jnp.exp2(m0 - m1)
        p = jnp.exp2(s * SCALE - m1[:1])
        l_all[qb] = l_all[qb] * factor + jnp.sum(p, axis=0, keepdims=True)
        m_all[qb] = m1
        values = vx[pl.ds(pl.multiple_of(item_tile[k] * TILE, TILE), TILE), :]
        acc_all[qb] = acc_all[qb] * factor[:1] + lax.dot_general(
            values, p.astype(jnp.bfloat16), TN, preferred_element_type=jnp.float32
        )

    @pl.when(items > 0)
    def _():
        scores(s_a, top_a, 0, 0)

        def pair(j, c):
            k = 2 * j
            scores(s_b, top_b, k + 1, k)
            absorb(s_a, top_a, k)
            scores(s_a, top_a, k + 2, k + 1)
            absorb(s_b, top_b, k + 1)
            return c

        lax.fori_loop(0, (items - 1) // 2, pair, 0)

        @pl.when(items % 2 == 0)
        def _():
            scores(s_b, top_b, items - 1, items - 2)
            absorb(s_a, top_a, items - 2)
            top_a[...] = top_b[...]

            def hand(i, c):
                rows = pl.ds(pl.multiple_of(i * 64, 64), 64)
                s_a[rows, :] = s_b[rows, :]
                return c

            lax.fori_loop(0, TILE // 64, hand, 0)

        absorb(s_a, top_a, items - 1)

    for qb in range(n_query):
        if last:
            total = l_all[qb]
            some = total > 0.0
            safe = jnp.where(some, total, 1.0)
            logsum = jnp.where(some, m_all[qb] + jnp.log2(safe), NEG)
            high = logsum.astype(jnp.bfloat16)
            rest = logsum - high.astype(jnp.float32)
            mid = rest.astype(jnp.bfloat16)
            low = (rest - mid.astype(jnp.float32)).astype(jnp.bfloat16)
            row = lax.broadcasted_iota(jnp.int32, (16, ROWS), 0)
            h2, m2, l2 = (jnp.concatenate([v, v], 0).astype(jnp.float32) for v in (high, mid, low))
            outs[qb][:D, :] = (acc_all[qb] / safe[:1]).astype(jnp.bfloat16)
            outs[qb][D:, :] = jnp.where(row == 0, h2, jnp.where(row == 1, m2, l2)).astype(jnp.bfloat16)
        else:
            outs[3 * qb][...], outs[3 * qb + 1][...] = m_all[qb], l_all[qb]

            def keep(i, carry, qb=qb):
                rows = pl.ds(pl.multiple_of(i * 64, 64), 64)
                outs[3 * qb + 2][rows, :] = acc_all[qb, rows, :]
                return carry

            lax.fori_loop(0, D // 64, keep, 0)


def run_chunk(work, steps, state, last, table, queries, messages):
    first = work[0] not in state
    sets = sorted({g for g, _ in work})
    n_query = len(work)
    n_keys = 256 * 2 * len(steps)
    keep = n_keys + TILE + 128
    max_items = n_query * (n_keys // TILE + 1) + 2
    shapes = [(8, ROWS), (8, ROWS), (D, ROWS)]
    smem = pl.BlockSpec(memory_space=pltpu.SMEM)
    vmem = pl.BlockSpec(memory_space=VMEM)
    operands = [table, *(queries[g] for g in sets), *messages]
    if not first:
        operands += [array for key in work for array in state[key]]
    if last:
        out_shape = [jax.ShapeDtypeStruct((OUT_ROWS, ROWS), jnp.bfloat16)] * n_query
    else:
        out_shape = [jax.ShapeDtypeStruct(s, jnp.float32) for s in shapes] * n_query
    pairs = n_query * n_keys * ROWS * 6 // 10
    name = "_".join(["attend", *(str(g) + "AB"[role] for g, role in work), str(len(steps))])
    results = pl.pallas_call(
        functools.partial(attend_chunk, tuple(work), tuple(sets), tuple(steps), first, last),
        out_shape=out_shape,
        in_specs=[smem] + [vmem] * (len(operands) - 1),
        out_specs=[vmem] * len(out_shape),
        scratch_shapes=[VMEM((n_query, *s), jnp.float32) for s in shapes]
        + [
            VMEM((n_query, ROWS, 2 * D), jnp.bfloat16),
            VMEM((keep, 2 * D), jnp.bfloat16),
            VMEM((keep, D), jnp.bfloat16),
            VMEM((TILE, ROWS), jnp.float32),
            VMEM((TILE, ROWS), jnp.float32),
            VMEM((8, ROWS), jnp.float32),
            VMEM((8, ROWS), jnp.float32),
            pltpu.SMEM((8,), jnp.int32),
            pltpu.SMEM((8,), jnp.int32),
            pltpu.SMEM((max_items,), jnp.int32),
            pltpu.SMEM((max_items,), jnp.int32),
        ],
        compiler_params=pltpu.CompilerParams(vmem_limit_bytes=24 * 2**20),
        cost_estimate=pl.CostEstimate(
            flops=1024 if sets == [0] else pairs * 1024, bytes_accessed=1024 if sets == [0] else 8 * 2**20, transcendentals=0
        ),
        name=name,
    )(*operands)
    if last:
        return results
    for i, key in enumerate(work):
        state[key] = tuple(results[3 * i : 3 * i + 3])
    return state


def project_body(table_ref, a_ref, b_ref, c_ref, d_ref, w_ref, give_ref, mine_ref, att):
    parts = (a_ref, b_ref, c_ref, d_ref)
    logs = []
    for part in parts:
        row = part[D:, :].astype(jnp.float32)
        logs.append(row[0:1] + row[1:2] + row[2:3])
    top = functools.reduce(jnp.maximum, logs)
    weights = [jnp.exp2(v - top) for v in logs]
    share = 1.0 / sum(weights)
    mixed = sum(part[:D, :].astype(jnp.float32) * (w * share) for part, w in zip(parts, weights))
    turned = mixed.T.astype(jnp.bfloat16)
    for h in range(HEADS):
        att[:, h * D : (h + 1) * D] = turned[h * BLK : (h + 1) * BLK, :]
    core = table_ref[PLACE + 4]
    half = BLK // 2
    wide = 1024

    def columns(c, carry):
        cols = pl.ds(pl.multiple_of(c * wide, wide), wide)
        full = jnp.dot(att[...], w_ref[:, cols], preferred_element_type=jnp.float32)
        give_ref[:, cols] = jnp.where(core == 0, full[half:], full[:half]).astype(jnp.bfloat16)
        mine_ref[:, cols] = jnp.where(core == 0, full[:half], full[half:])
        return carry

    lax.fori_loop(0, w_ref.shape[1] // wide, columns, 0)


def project(table, parts, weight):
    vmem = pl.BlockSpec(memory_space=VMEM)
    wide = weight.shape[1]
    return pl.pallas_call(
        project_body,
        out_shape=(
            jax.ShapeDtypeStruct((BLK // 2, wide), jnp.bfloat16),
            jax.ShapeDtypeStruct((BLK // 2, wide), jnp.float32),
        ),
        in_specs=[pl.BlockSpec(memory_space=pltpu.SMEM)] + [vmem] * 5,
        out_specs=(vmem, vmem),
        scratch_shapes=[VMEM((BLK, HEADS * D), jnp.bfloat16)],
        compiler_params=pltpu.CompilerParams(vmem_limit_bytes=24 * 2**20),
        cost_estimate=pl.CostEstimate(flops=2 * BLK * HEADS * D * wide, bytes_accessed=12 * 2**20, transcendentals=0),
        name="project",
    )(table, *parts, weight)


def total_body(a_ref, b_ref, out):
    out[...] = (a_ref[...].astype(jnp.float32) + b_ref[...].astype(jnp.float32)).astype(out.dtype)


def total(a, b, dtype):
    vmem = pl.BlockSpec(memory_space=VMEM)
    return pl.pallas_call(
        total_body,
        out_shape=jax.ShapeDtypeStruct(a.shape, dtype),
        in_specs=[vmem] * 2,
        out_specs=vmem,
        compiler_params=pltpu.CompilerParams(vmem_limit_bytes=8 * 2**20),
        name="total",
    )(a, b)


def stage_body(src, dst):
    dst[...] = src[...]


def stage(array):
    vmem = pl.BlockSpec(memory_space=VMEM)
    return pl.pallas_call(
        stage_body,
        out_shape=jax.ShapeDtypeStruct(array.shape, array.dtype),
        in_specs=[vmem],
        out_specs=vmem,
        compiler_params=pltpu.CompilerParams(vmem_limit_bytes=8 * 2**20),
        name="stage",
    )(array)


def on_device(queries, window_keys, window_values, stored_keys, stored_values, block_order, window_offset, out_weight):
    x, yl, z = lax.axis_index("x"), lax.axis_index("yl"), lax.axis_index("z")
    core, yh = lax.axis_index("core"), lax.axis_index("yh")
    place = jnp.stack([x, yl, z, window_offset[0], core, yh]).astype(jnp.int32)
    table = jnp.concatenate([block_order, place])
    shard = jnp.concatenate([window_keys, stored_keys, window_values, stored_values], 0)

    def along(array, axis, size, to):
        return lax.ppermute(array, axis, [(i, to(i)) for i in range(size)])

    shard, queries = lax.optimization_barrier((shard, queries))
    other = along(shard, "x", 4, lambda i: 3 - i)
    base = jnp.concatenate([shard, other], 0)
    pair = [(a, b) for a in range(4) for b in range(2)]
    both = [(2 * a + b, 2 * (a ^ 1) + (1 - b)) for a, b in pair]
    to_member = [
        lambda v: v,
        lambda v: along(v, "x", 4, lambda i: i ^ 1),
        lambda v: along(v, "yl", 2, lambda i: 1 - i),
        lambda v: lax.ppermute(v, ("x", "yl"), both),
    ]
    q_sets = [queries] + [to_member[g](queries) for g in (1, 2, 3)]
    up = lambda a: along(a, "z", 8, lambda i: (i + 1) % 8)
    down = lambda a: along(a, "z", 8, lambda i: (i - 1) % 8)
    base, table, q_sets[0] = lax.optimization_barrier((base, table, stage(queries)))
    a1, b1 = up(base), down(base)
    a2, b2 = up(a1), down(b1)
    state = {}
    run = lambda work, steps, messages, last=False: run_chunk(work, steps, state, last, table, q_sets, messages)
    tie = lax.optimization_barrier
    near = (0, -1, 1), (base, a1, b1)
    A, B = 0, 1
    run([(0, A), (0, B)], *near)
    run([(3, A), (3, B)], *near)
    a2, b2, state[0, A], state[3, A] = tie((a2, b2, state[0, A], state[3, A]))
    a3, b3 = up(a2), down(b2)
    far = jnp.concatenate([up(a3[:SHARD]), down(b3[SHARD:])], 0)
    run([(1, A), (1, B), (2, A), (2, B)], *near)
    run([(g, r) for r in (A, B) for g in (1, 2, 3)], (-2, 2), (a2, b2))
    end = (-3, 3, 4), (a3, b3, far)
    sent_a = run([(3, A), (1, A), (2, A)], *end, True)
    *sent_a, state[3, B] = tie((*sent_a, state[3, B]))
    got_a = [to_member[g](v) for g, v in zip((3, 1, 2), sent_a)]
    sent_b = run([(3, B), (1, B), (2, B)], *end, True)
    *sent_b, state[0, A] = tie((*sent_b, state[0, A]))
    got_b = [to_member[g](v) for g, v in zip((3, 1, 2), sent_b)]
    rest = (-2, 2, -3, 3, 4), (a2, b2, a3, b3, far)
    (own_a,) = run([(0, A)], *rest, True)
    swap = lambda v, axis: along(v, axis, 2, lambda i: 1 - i)
    give_a, keep_a = project(table, (own_a, *got_a), out_weight)
    give_a, *got_b = tie((give_a, *got_b))
    sum_a = total(keep_a, swap(give_a, "core"), jnp.bfloat16)
    sum_a, state[0, B] = tie((sum_a, state[0, B]))
    across = swap(sum_a, "yh")
    (own_b,) = run([(0, B)], *rest, True)
    give_b, keep_b = project(table, (own_b, *got_b), out_weight)
    keep_b = total(keep_b, across, jnp.float32)
    return (keep_b + swap(give_b, "core").astype(jnp.float32)).astype(jnp.bfloat16)


def solution(mesh):
    fine = Mesh(mesh.devices.reshape(4, 2, 8, 2, 2), ("x", "yl", "z", "yh", "core"))
    ctx, tp = ("x", "yl", "z"), ("yh", "core")
    return jax.shard_map(
        on_device,
        mesh=fine,
        in_specs=(P(ctx, tp),) * 5 + (P(), P(), P(tp, None)),
        out_specs=P((*ctx, *tp), None),
        check_vma=False,
    )
```
